128 devices in a mesh: sib: 2 (over x_lo), row: 8 (over y, core), col: 8 (over z, x_hi).
Axes of the slice: x: 4 (x_hi: 2, x_lo: 2; x = x_hi * 2 + x_lo), y: 4, z: 4, core: 2. Of those that a mesh axis runs over, the one named last changes fastest.
Arguments:
- child_tiles: float32 [2, 64, 128, 128, 128], P('sib', ('row', 'col')), may hold values from -6 to 6
- child_rows: int32 [2, 64], P('sib'), may hold values from 0 to 127, as said below
- child_slots: int32 [2, 64, 128], P('sib', ('row', 'col')), may hold values from 0 to 4095, as said below
- tile_count: int32 [2, 64], P('sib', ('row', 'col')), may hold values from 64 to 128, as said below
- inverses: float32 [2, 512, 512], replicated, as said below
Outputs:
- factored: float32 [8, 16, 16, 8, 128, 128], P(None, ('sib', 'row'), None, 'col')
The draws below stay inside these ranges and needn't reach their ends.
Inputs may be any that keep to these rules, and one draw needn't show every extreme that they name: `child_rows`: A child's entries are distinct; entry i leaves the same remainder as i when divided by the number of grid rows of the parent. `child_slots`: call the owner of parent tile (I, J) the grid row I mod (number of grid rows) and grid column J mod (number of grid columns). Among the live slots of one device at most 2 carry tiles with one owner; in every draw some device reaches 2 for some owner. `tile_count`: some device of each child has all 128 slots live. `inverses`: each matrix is lower triangular with positive diagonal.
All inputs are finite; a program needn't handle non-finite values.
Results may differ from the reference program's by a relative error of at most 0.00012.
Values sent between devices are 32-bit elements; how exact they have to be, the bound alone decides.
No kernel may reach another device: no remote copies, remote signals or barrier semaphores. Data moves between devices by JAX's collectives and lax.ppermute only.
A program may use at most 192 MiB of HBM per device.

```python
import math
import jax
import jax.numpy as jnp
from jax import lax

NF = 16384
TILE = 128
PANEL = 512
NPANEL = 2
CHILD_TILES = 64
CAP = 2
TSLOT = 128
N_SIB = 2
N_ROW = 8
N_COL = 8


def draw_child_rows(key, part):
    key = jax.random.fold_in(key, 11)
    grid = N_SIB * N_ROW
    per_residue = CHILD_TILES // grid
    subkeys = jax.random.split(key, N_SIB * grid)
    shuffled = jax.vmap(lambda k: jax.random.permutation(k, NF // TILE // grid))(subkeys)[:, :per_residue]
    quotient = shuffled.reshape(N_SIB, grid, per_residue).transpose(0, 2, 1)
    residue = jnp.arange(grid, dtype=jnp.int32)
    return (residue[None, None, :] + grid * quotient).reshape(N_SIB, CHILD_TILES).astype(jnp.int32)


def slots_of_device(k):
    grid = N_SIB * N_ROW
    owners_all = grid * N_COL
    pieces = jax.random.split(k, 4)
    owners = jax.random.permutation(pieces[0], owners_all)[:TSLOT // CAP]
    owners = jax.random.permutation(pieces[1], jnp.repeat(owners, CAP))
    owner_row = owners // N_COL
    owner_col = owners % N_COL
    i = owner_row + grid * jax.random.randint(pieces[2], (TSLOT,), 0, CHILD_TILES // grid)
    j = owner_col + N_COL * jax.random.randint(pieces[3], (TSLOT,), 0, CHILD_TILES // N_COL)
    return i * CHILD_TILES + j


def draw_child_slots(key, part):
    key = jax.random.fold_in(key, 12)
    subkeys = jax.random.split(key, N_SIB * N_ROW * N_COL)
    return jax.vmap(slots_of_device)(subkeys).reshape(N_SIB, N_ROW * N_COL, TSLOT).astype(jnp.int32)


def draw_tile_count(key, part):
    key = jax.random.fold_in(key, 13)
    pieces = jax.random.split(key, 2)
    counts = jax.random.randint(pieces[0], (N_SIB, N_ROW * N_COL), TSLOT // 2, TSLOT + 1)
    fullest = jax.random.randint(pieces[1], (N_SIB,), 0, N_ROW * N_COL)
    device_ids = jnp.arange(N_ROW * N_COL, dtype=jnp.int32)
    counts = jnp.where(device_ids[None, :] == fullest[:, None], TSLOT, counts)
    return counts.astype(jnp.int32)


def draw_inverses(key, part):
    key = jax.random.fold_in(key, 14)
    pieces = jax.random.split(key, 2)
    diagonal_part = jnp.exp(jax.random.uniform(pieces[0], (NPANEL, PANEL), jnp.float32, math.log(0.05), math.log(0.2)))
    noise_values = jax.random.normal(pieces[1], (NPANEL, PANEL, PANEL), jnp.float32)
    strict = jnp.tril(jnp.ones((PANEL, PANEL), jnp.float32), -1)
    identity = jnp.eye(PANEL, dtype=jnp.float32)
    result = noise_values * (0.1 / math.sqrt(PANEL)) * strict[None] + diagonal_part[:, :, None] * identity[None]
    return result.astype(jnp.float32)


def shard_levels(stream_key, extent, cuts, least, high):
    factor_of, own = 1.0, jax.random.fold_in(stream_key, 6)
    for position, blocks in cuts:
        steps = jnp.exp(jax.random.uniform(jax.random.fold_in(own, position), (blocks,), jnp.float32, least / len(cuts), high / len(cuts)))
        factor_of = factor_of * jnp.repeat(steps, extent[position] // blocks).reshape([-1 if axis == position else 1 for axis in range(len(extent))])
    return factor_of


def noise(stream_key, dims, deviation, most, cuts=(), kind=jnp.bfloat16):
    factor_of = shard_levels(stream_key, dims, cuts, -0.22, 0.18) if cuts else 1.0
    values = jax.random.normal(stream_key, dims, jnp.float32) * deviation * factor_of
    return jnp.minimum(jnp.maximum(values, -most), most).astype(kind)


def setup_inputs(seed: int = 0) -> dict:
    arg_keys = jax.random.split(jax.random.key(seed), 6)
    return {
        "child_tiles": noise(arg_keys[0], (N_SIB, N_ROW * N_COL, TSLOT, TILE, TILE), 1.0, 6.0, ((0, 2), (1, 64)), jnp.float32),
        "child_rows": draw_child_rows(jax.random.fold_in(arg_keys[5], 71), 0),
        "child_slots": draw_child_slots(jax.random.fold_in(arg_keys[5], 71), 0),
        "tile_count": draw_tile_count(jax.random.fold_in(arg_keys[5], 71), 0),
        "inverses": draw_inverses(jax.random.fold_in(arg_keys[5], 71), 0),
    }


def reference(child_tiles, child_rows, child_slots, tile_count, inverses):
    tile_order = NF // TILE
    grid_rows = N_SIB * N_ROW
    front_tiles = jnp.zeros((tile_order, tile_order, TILE, TILE), jnp.float32)
    for child_index in range(N_SIB):
        tile_data = child_tiles[child_index].reshape(-1, TILE, TILE)
        slot_order = jnp.arange(TSLOT, dtype=jnp.int32)
        is_live = (slot_order[None, :] < tile_count[child_index][:, None]).reshape(-1)
        slot_ids = child_slots[child_index].reshape(-1)
        row_list = child_rows[child_index]
        parent_row = row_list[slot_ids // CHILD_TILES]
        parent_col = row_list[slot_ids % CHILD_TILES]
        weighted = tile_data * is_live.astype(jnp.float32)[:, None, None]
        front_tiles = front_tiles.at[parent_row, parent_col].add(weighted)
    matrix = front_tiles.transpose(0, 2, 1, 3).reshape(NF, NF)
    for panel_step in range(NPANEL):
        start = panel_step * PANEL
        finish = start + PANEL
        factor = jnp.dot(matrix[finish:, start:finish], inverses[panel_step].T, precision=lax.Precision.HIGHEST)
        matrix = matrix.at[finish:, start:finish].set(factor)
        update = jnp.dot(factor, factor.T, precision=lax.Precision.HIGHEST)
        matrix = matrix.at[finish:, finish:].add(-update)
    result_tiles = matrix.reshape(tile_order, TILE, tile_order, TILE).transpose(0, 2, 1, 3)
    return result_tiles.reshape(tile_order // grid_rows, grid_rows, tile_order // N_COL, N_COL, TILE, TILE)
```

```python
import functools

import jax
import jax.numpy as jnp
from jax import lax
from jax.experimental import pallas as pl
from jax.experimental.pallas import tpu as pltpu
from jax.sharding import PartitionSpec as P

NF = 16384
TILE = 128
PANEL = 512
NPANEL = 2
CHILD_TILES = 64
CAP = 2
PT = PANEL // TILE
WIDE = NPANEL * PANEL
META = 8
LROWS, LCOLS = 8, 16
f32, bf16, i32 = jnp.float32, jnp.bfloat16, jnp.int32
MIB = 1 << 20


def split(x):
    hi = x.astype(bf16)
    return hi, (x - hi.astype(f32)).astype(bf16)


def dot3(a, b):
    dims = (((1,), (1,)), ((), ()))
    mul = lambda u, v: lax.dot_general(u, v, dims, preferred_element_type=f32)
    return mul(a[0], b[0]) + (mul(a[0], b[1]) + mul(a[1], b[0]))


def pack_kernel(place, live, tiles, meta, out, sem, meta_sem):
    head = pltpu.make_async_copy(meta, out.at[:, CAP * TILE :, :], meta_sem)
    head.start()

    def copy(m):
        d = place[m] // CAP
        k = place[m] % CAP
        return pltpu.make_async_copy(
            tiles.at[m], out.at[d, pl.ds(pl.multiple_of(k * TILE, TILE), TILE), :], sem
        )

    lax.fori_loop(0, live[0], lambda m, c: (copy(m).start(), c)[1], 0)
    lax.fori_loop(0, live[0], lambda m, c: (copy(m).wait(), c)[1], 0)
    head.wait()


def pack(place, live, tiles, meta):
    devices = meta.shape[0]
    return pl.pallas_call(
        pack_kernel,
        out_shape=jax.ShapeDtypeStruct((devices, CAP * TILE + META, TILE), f32),
        in_specs=[
            pl.BlockSpec(memory_space=pltpu.SMEM),
            pl.BlockSpec(memory_space=pltpu.SMEM),
            pl.BlockSpec(memory_space=pl.ANY),
            pl.BlockSpec(memory_space=pltpu.VMEM),
        ],
        out_specs=pl.BlockSpec(memory_space=pl.ANY),
        scratch_shapes=[pltpu.SemaphoreType.DMA, pltpu.SemaphoreType.DMA],
        compiler_params=pltpu.CompilerParams(vmem_limit_bytes=16 * MIB),
        name="pack",
    )(place, live, tiles, meta)


def add_kernel(panel, landing, arrived, out, buf, where_to, sem):
    slots = landing.shape[0]

    def fetch(k, n):
        pair, turn = k // CAP, k % CAP
        rows = pl.ds(pl.multiple_of(turn * TILE, TILE), TILE)
        return pltpu.make_async_copy(arrived.at[pair, rows, :], buf.at[n], sem)

    def scan(k, n):
        t = landing[k]
        hit = (t >= 0) & (t % LCOLS == 0) if panel else t >= 0

        @pl.when(hit)
        def _():
            where_to[n] = t
            fetch(k, n).start()

        return n + hit.astype(i32)

    count = lax.fori_loop(0, slots, scan, 0)
    out[...] = jnp.zeros_like(out)
    lax.fori_loop(0, count, lambda n, c: (fetch(0, n).wait(), c)[1], 0)

    def add(n, c):
        t = where_to[n]
        if panel:
            a = t // LCOLS
            out[a] = out[a] + buf[n]
        else:
            a, b = t // LCOLS, t % LCOLS
            out[a, b] = out[a, b] + buf[n]
        return c

    lax.fori_loop(0, count, add, 0)


def add_up(panel, landing, arrived):
    slots = landing.shape[0]
    shape = (LROWS, TILE, TILE) if panel else (LROWS, LCOLS, TILE, TILE)
    return pl.pallas_call(
        functools.partial(add_kernel, panel),
        out_shape=jax.ShapeDtypeStruct(shape, f32),
        in_specs=[
            pl.BlockSpec(memory_space=pltpu.SMEM),
            pl.BlockSpec(memory_space=pl.ANY),
        ],
        out_specs=pl.BlockSpec(memory_space=pltpu.VMEM),
        scratch_shapes=[
            pltpu.VMEM((slots, TILE, TILE), f32),
            pltpu.SMEM((slots,), i32),
            pltpu.SemaphoreType.DMA,
        ],
        compiler_params=pltpu.CompilerParams(vmem_limit_bytes=40 * MIB),
        cost_estimate=pl.CostEstimate(
            flops=1000, bytes_accessed=MIB if panel else 24 * MIB, transcendentals=0
        ),
        name="add_panel" if panel else "add_all",
    )(landing, arrived)


def times(x, w):
    half = PANEL // 2
    left = dot3([u[:, :half] for u in x], [v[:half, :half] for v in w])
    right = dot3(x, [v[half:, :] for v in w])
    return jnp.concatenate([left, right], axis=1)


def factor(a, inv, low):
    first = times(split(a[:, :PANEL]), inv[0])
    rest = a[:, PANEL:] - dot3(split(first), low)
    return first, times(split(rest), inv[1])


CHUNK = 256


def rows_kernel(at, *refs):
    pieces, corner, inverses = refs[:8], refs[8], refs[9]
    l_hi, l_lo, l_own, inv_hi, inv_lo, low_hi, low_lo = refs[10:17]
    raw, own_f32, square = refs[17:20]
    sib, y, core, z, xh = (at[i] for i in range(5))
    my_row = (sib * 4 + y) * 2 + core
    my_col = z * 2 + xh
    sources = [
        my_col,
        z * 2 + 1 - xh,
        (z + 3) % 4 * 2 + xh,
        (z + 1) % 4 * 2 + xh,
        (z + 3) % 4 * 2 + 1 - xh,
        (z + 1) % 4 * 2 + 1 - xh,
        (z + 2) % 4 * 2 + xh,
        (z + 2) % 4 * 2 + 1 - xh,
    ]
    for piece, source in zip(pieces, sources):
        lanes = pl.ds(pl.multiple_of(source * TILE, TILE), TILE)
        for a in range(LROWS):
            raw[a * TILE : (a + 1) * TILE, lanes] = piece[a]
    for p in range(NPANEL):
        hi, lo = split(inverses[p])
        inv_hi[p] = hi
        inv_lo[p] = lo
    inv = [(inv_hi[p], inv_lo[p]) for p in range(NPANEL)]

    y_bit = jnp.where(y >= 2, y, 3 - y) % 2
    z_bit = jnp.where(z < 2, z, 3 - z)
    for q in range(16):
        yb = y_bit ^ (q & 1)
        zb = z_bit ^ (q >> 1 & 1)
        xb = xh ^ (q >> 2 & 1)
        cb = core ^ (q >> 3 & 1)
        r = pl.multiple_of((yb * 2 + cb) * TILE, TILE)
        c = pl.multiple_of((zb * 2 + xb) * TILE, TILE)
        square[pl.ds(r, TILE), pl.ds(c, TILE)] = corner[q]

    low_hi[...], low_lo[...] = split(times(split(square[...]), inv[0]))

    def chunk(i, carry):
        rows = pl.ds(pl.multiple_of(i * CHUNK, CHUNK), CHUNK)
        inv = [(inv_hi[p], inv_lo[p]) for p in range(NPANEL)]
        first, second = factor(raw[rows, :], inv, (low_hi[...], low_lo[...]))
        own_f32[rows, :PANEL] = first
        own_f32[rows, PANEL:] = second
        row_tile = jnp.where(
            (i == 0) & (lax.broadcasted_iota(i32, (CHUNK, 1), 0) < TILE), my_row, NF
        )
        first = jnp.where(row_tile >= PT, first, 0.0)
        second = jnp.where(row_tile >= 2 * PT, second, 0.0)
        hi, lo = split(first)
        l_hi[rows, :PANEL] = hi
        l_lo[rows, :PANEL] = lo
        hi, lo = split(second)
        l_hi[rows, PANEL:] = hi
        l_lo[rows, PANEL:] = lo
        return carry

    lax.fori_loop(0, LROWS * TILE // CHUNK, chunk, 0)
    lanes = pl.ds(pl.multiple_of(my_col * TILE, TILE), TILE)
    for a in range(LROWS):
        l_own[a] = own_f32[a * TILE : (a + 1) * TILE, lanes]


def rows_factor(at, pieces, corner, inverses):
    vmem = pl.BlockSpec(memory_space=pltpu.VMEM)
    height = LROWS * TILE
    shapes = [
        ((height, WIDE), bf16),
        ((height, WIDE), bf16),
        ((LROWS, TILE, TILE), f32),
        ((NPANEL, PANEL, PANEL), bf16),
        ((NPANEL, PANEL, PANEL), bf16),
        ((PANEL, PANEL), bf16),
        ((PANEL, PANEL), bf16),
    ]
    return pl.pallas_call(
        rows_kernel,
        out_shape=[jax.ShapeDtypeStruct(s, t) for s, t in shapes],
        in_specs=[pl.BlockSpec(memory_space=pltpu.SMEM)] + [vmem] * 10,
        out_specs=[vmem] * 7,
        scratch_shapes=[
            pltpu.VMEM((height, WIDE), f32),
            pltpu.VMEM((height, WIDE), f32),
            pltpu.VMEM((PANEL, PANEL), f32),
        ],
        compiler_params=pltpu.CompilerParams(vmem_limit_bytes=48 * MIB),
        cost_estimate=pl.CostEstimate(
            flops=6_000_000_000, bytes_accessed=14 * MIB, transcendentals=0
        ),
        name="rows_factor",
    )(at, *pieces, corner, inverses)


def update_kernel(
    at, column, front, l_hi, l_lo, l_own, inv_hi, inv_lo, low_hi, low_lo, out, raw, c_hi, c_lo
):
    step = pl.program_id(0)
    sib, y, core, z, xh = (at[i] for i in range(5))
    my_row = (sib * 4 + y) * 2 + core
    my_col = z * 2 + xh
    for s in range(2):
        for py in range(4):
            for pc in range(2):
                source = (py - z + 4) % 4 * 2 + pc
                lanes = pl.ds(pl.multiple_of(source * TILE, TILE), TILE)
                raw[s * TILE : (s + 1) * TILE, lanes] = column[(s * 4 + py) * 2 + pc, 0]
    inv = [(inv_hi[p], inv_lo[p]) for p in range(NPANEL)]
    first, second = factor(raw[...], inv, (low_hi[...], low_lo[...]))
    col_tile = jnp.where(
        (step == 0) & (lax.broadcasted_iota(i32, (2 * TILE, 1), 0) < TILE), my_col, NF
    )
    first = jnp.where(col_tile >= PT, first, 0.0)
    second = jnp.where(col_tile >= 2 * PT, second, 0.0)
    hi, lo = split(first)
    c_hi[:, :PANEL] = hi
    c_lo[:, :PANEL] = lo
    hi, lo = split(second)
    c_hi[:, PANEL:] = hi
    c_lo[:, PANEL:] = lo

    def rows(i, carry):
        here = pl.ds(pl.multiple_of(i * CHUNK, CHUNK), CHUNK)
        change = dot3((l_hi[here, :], l_lo[here, :]), (c_hi[...], c_lo[...]))
        for p in range(CHUNK // TILE):
            for b in range(2):
                piece = change[p * TILE : (p + 1) * TILE, b * TILE : (b + 1) * TILE]
                t = i * (CHUNK // TILE) + p
                out[t, b] = front[t, b] - piece
        return carry

    lax.fori_loop(0, LROWS * TILE // CHUNK, rows, 0)

    @pl.when(step == 0)
    def _():
        for t in range(1, LROWS):
            out[t, 0] = l_own[t]

        @pl.when((my_row >= 2 * PT) | ((my_row >= PT) & (my_col < PT)))
        def _():
            out[0, 0] = l_own[0]


def update(at, column, front, l_hi, l_lo, l_own, inv_hi, inv_lo, low_hi, low_lo):
    height = LROWS * TILE
    whole = lambda x: pl.BlockSpec(x.shape, lambda j: (0,) * x.ndim)
    block = pl.BlockSpec((LROWS, 2, TILE, TILE), lambda j: (0, j, 0, 0))
    return pl.pallas_call(
        update_kernel,
        grid=(LCOLS // 2,),
        out_shape=jax.ShapeDtypeStruct((LROWS, LCOLS, TILE, TILE), f32),
        in_specs=[
            pl.BlockSpec(memory_space=pltpu.SMEM),
            pl.BlockSpec((16, 1, TILE, TILE), lambda j: (0, j, 0, 0)),
            block,
        ]
        + [whole(x) for x in (l_hi, l_lo, l_own, inv_hi, inv_lo, low_hi, low_lo)],
        out_specs=block,
        scratch_shapes=[
            pltpu.VMEM((2 * TILE, WIDE), f32),
            pltpu.VMEM((2 * TILE, WIDE), bf16),
            pltpu.VMEM((2 * TILE, WIDE), bf16),
        ],
        compiler_params=pltpu.CompilerParams(vmem_limit_bytes=48 * MIB),
        cost_estimate=pl.CostEstimate(
            flops=22_000_000_000, bytes_accessed=30 * MIB, transcendentals=0
        ),
        name="update",
    )(at, column, front, l_hi, l_lo, l_own, inv_hi, inv_lo, low_hi, low_lo)


def move(x, axis, size, to):
    return lax.ppermute(x, axis, [(i, to(i)) for i in range(size)])


def gather_row(x):
    up, down = lambda c: (c + 2) % 8, lambda c: (c - 2) % 8
    other = move(x, "col", 8, lambda c: c ^ 1)
    x_up, x_down = move(x, "col", 8, up), move(x, "col", 8, down)
    other_up, other_down = move(other, "col", 8, up), move(other, "col", 8, down)
    x_far, other_far = move(x_up, "col", 8, up), move(other_down, "col", 8, down)
    return [x, other, x_up, x_down, other_up, other_down, x_far, other_far]


def gather_corner(tile):
    sib, row, col = (lax.axis_index(n) for n in ("sib", "row", "col"))
    other = lax.ppermute(tile, "sib", [(0, 1)])
    tile = jnp.where(sib == 0, tile, other)
    other = lax.ppermute(tile, "row", [(4, 2), (5, 3), (6, 0), (7, 1)])
    tile = jnp.where(row >= 4, tile, other)
    other = lax.ppermute(tile, "col", [(0, 6), (1, 7), (2, 4), (3, 5)])
    tiles = jnp.where(col < 4, tile, other)[None]
    for axis, bit in (("row", 2), ("col", 2), ("col", 1), ("row", 1)):
        got = move(tiles, axis, 8, lambda i: i ^ bit)
        tiles = jnp.concatenate([tiles, got], axis=0)
    return tiles


def gather_column(x):
    moves = []
    for y in range(4):
        for core in range(2):
            for z in range(4):
                for xh in range(2):
                    to = ((y + z) % 4 * 2 + xh) * 8 + y * 2 + core
                    moves.append(((y * 2 + core) * 8 + z * 2 + xh, to))
    return lax.all_gather(lax.ppermute(x, ("row", "col"), moves), ("sib", "row"))


def local(child_tiles, child_rows, child_slots, tile_count, inverses):
    grid_rows = lax.axis_size("sib") * lax.axis_size("row")
    columns = lax.axis_size("col")
    devices = grid_rows * columns
    slot_ids = child_slots[0, 0]
    live = tile_count[0]
    row_list = child_rows[0]
    child_row, child_col = slot_ids // CHILD_TILES, slot_ids % CHILD_TILES
    positions = jnp.arange(CHILD_TILES, dtype=i32)
    lookup = lambda x: jnp.sum(
        jnp.where(x[:, None] == positions[None, :], row_list[None, :], 0), axis=1
    )
    parent_row, parent_col = lookup(child_row), lookup(child_col)
    owner = parent_row % grid_rows * columns + parent_col % columns
    target = parent_row // grid_rows * LCOLS + parent_col // columns
    order = jnp.arange(slot_ids.shape[0], dtype=i32)
    is_live = order < live
    earlier = (
        (owner[:, None] == owner[None, :])
        & is_live[None, :]
        & (order[None, :] < order[:, None])
    )
    rank = jnp.sum(earlier.astype(i32), axis=1)
    place = jnp.where(is_live, owner * CAP + rank, devices * CAP)
    filled = place[None, :] == jnp.arange(devices * CAP, dtype=i32)[:, None]
    destined = jnp.sum(jnp.where(filled, target[None, :] + 1, 0), axis=1) - 1
    meta = jnp.broadcast_to(
        destined.astype(f32).reshape(devices, CAP, 1, 1),
        (devices, CAP, META // CAP, TILE),
    ).reshape(devices, META, TILE)
    outgoing = pack(place, live, child_tiles[0, 0], meta)
    arrived = lax.all_to_all(
        outgoing, ("sib", "row", "col"), split_axis=0, concat_axis=0, tiled=True
    )
    landing = arrived[:, CAP * TILE :: META // CAP, 0].astype(i32).reshape(-1)

    panel = add_up(True, landing, arrived)
    column = gather_column(panel)
    pieces = gather_row(panel)
    corner = gather_corner(panel[0])
    row = lax.axis_index("row")
    col = lax.axis_index("col")
    at = jnp.stack([lax.axis_index("sib"), row // 2, row % 2, col // 2, col % 2])
    at = at.astype(i32)
    front = add_up(False, landing, arrived)
    known = rows_factor(at, pieces, corner, inverses)
    out = update(at, column, front, *known)
    return out.reshape(LROWS, 1, LCOLS, 1, TILE, TILE)


def solution(mesh):
    return jax.shard_map(
        local,
        mesh=mesh,
        in_specs=(
            P("sib", ("row", "col"), None, None, None),
            P("sib", None),
            P("sib", ("row", "col"), None),
            P("sib", ("row", "col")),
            P(),
        ),
        out_specs=P(None, ("sib", "row"), None, "col", None, None),
        check_vma=False,
    )
```

```python
import functools

import jax
import jax.numpy as jnp
from jax import lax
from jax.experimental import pallas as pl
from jax.experimental.pallas import tpu as pltpu
from jax.sharding import PartitionSpec as P

NF = 16384
TILE = 128
PANEL = 512
NPANEL = 2
CHILD_TILES = 64
CAP = 2
PT = PANEL // TILE
WIDE = NPANEL * PANEL
META = 8
LROWS, LCOLS = 8, 16
f32, bf16, i32 = jnp.float32, jnp.bfloat16, jnp.int32
MIB = 1 << 20


def split(x):
    hi = x.astype(bf16)
    return hi, (x - hi.astype(f32)).astype(bf16)


def pack_kernel(place, live, tiles, meta, out, sem, meta_sem):
    head = pltpu.make_async_copy(meta, out.at[:, CAP * TILE :, :], meta_sem)
    head.start()

    def copy(m):
        d = place[m] // CAP
        k = place[m] % CAP
        return pltpu.make_async_copy(
            tiles.at[m], out.at[d, pl.ds(pl.multiple_of(k * TILE, TILE), TILE), :], sem
        )

    lax.fori_loop(0, live[0], lambda m, c: (copy(m).start(), c)[1], 0)
    lax.fori_loop(0, live[0], lambda m, c: (copy(m).wait(), c)[1], 0)
    head.wait()


def pack(place, live, tiles, meta):
    devices = meta.shape[0]
    return pl.pallas_call(
        pack_kernel,
        out_shape=jax.ShapeDtypeStruct((devices, CAP * TILE + META, TILE), f32),
        in_specs=[
            pl.BlockSpec(memory_space=pltpu.SMEM),
            pl.BlockSpec(memory_space=pltpu.SMEM),
            pl.BlockSpec(memory_space=pl.ANY),
            pl.BlockSpec(memory_space=pltpu.VMEM),
        ],
        out_specs=pl.BlockSpec(memory_space=pl.ANY),
        scratch_shapes=[pltpu.SemaphoreType.DMA, pltpu.SemaphoreType.DMA],
        compiler_params=pltpu.CompilerParams(vmem_limit_bytes=16 * MIB),
        name="pack",
    )(place, live, tiles, meta)


def add_kernel(panel, *refs):
    if panel:
        arrived, out, landing, buf, where_to, sem, head, places, head_sem = refs
        slots = arrived.shape[0] * CAP
        copy = pltpu.make_async_copy(arrived.at[:, CAP * TILE :, :], head, head_sem)
        copy.start()
        copy.wait()
        places[...] = jnp.sum(head[...], axis=0).astype(i32) - 1
        copy = pltpu.make_async_copy(places, landing, head_sem)
        copy.start()
        out[...] = jnp.zeros_like(out)
        copy.wait()
    else:
        landing, arrived, out, buf, where_to, sem = refs
        slots = arrived.shape[0] * CAP

    def fetch(k, n):
        pair, turn = k // CAP, k % CAP
        rows = pl.ds(pl.multiple_of(turn * TILE, TILE), TILE)
        return pltpu.make_async_copy(arrived.at[pair, rows, :], buf.at[n], sem)

    def scan(k, n):
        t = landing[k % CAP, k // CAP]
        hit = (t >= 0) & (t % LCOLS == 0) if panel else t >= 0

        @pl.when(hit)
        def _():
            where_to[n] = t
            fetch(k, n).start()

        return n + hit.astype(i32)

    count = lax.fori_loop(0, slots, scan, 0)
    if not panel:
        out[...] = jnp.zeros_like(out)
    lax.fori_loop(0, count, lambda n, c: (fetch(0, n).wait(), c)[1], 0)

    def add(n, c):
        t = where_to[n]
        if panel:
            a = t // LCOLS
            out[a] = out[a] + buf[n]
        else:
            a, b = t // LCOLS, t % LCOLS
            out[a, b] = out[a, b] + buf[n]
        return c

    lax.fori_loop(0, count, add, 0)


def add_up(panel, arrived, landing=None):
    devices = arrived.shape[0]
    vmem = pl.BlockSpec(memory_space=pltpu.VMEM)
    smem = pl.BlockSpec(memory_space=pltpu.SMEM)
    scratch = [
        pltpu.VMEM((devices * CAP, TILE, TILE), f32),
        pltpu.SMEM((devices * CAP,), i32),
        pltpu.SemaphoreType.DMA,
    ]
    any_space = pl.BlockSpec(memory_space=pl.ANY)
    if panel:
        return pl.pallas_call(
            functools.partial(add_kernel, True),
            out_shape=[
                jax.ShapeDtypeStruct((LROWS, TILE, TILE), f32),
                jax.ShapeDtypeStruct((META, devices), i32),
            ],
            in_specs=[any_space],
            out_specs=[vmem, smem],
            scratch_shapes=scratch
            + [
                pltpu.VMEM((devices, META, TILE), f32),
                pltpu.VMEM((META, devices), i32),
                pltpu.SemaphoreType.DMA,
            ],
            compiler_params=pltpu.CompilerParams(vmem_limit_bytes=56 * MIB),
            name="add_panel",
        )(arrived)
    return pl.pallas_call(
        functools.partial(add_kernel, False),
        out_shape=jax.ShapeDtypeStruct((LROWS, LCOLS, TILE, TILE), f32),
        in_specs=[smem, any_space],
        out_specs=vmem,
        scratch_shapes=scratch,
        compiler_params=pltpu.CompilerParams(vmem_limit_bytes=30 * MIB),
        cost_estimate=pl.CostEstimate(
            flops=1000, bytes_accessed=24 * MIB, transcendentals=0
        ),
        name="add_all",
    )(landing, arrived)


BLOCK = 256
KP = 3 * PANEL


def left_form(ref, rows, lane, x):
    hi, lo = split(x)
    for k in range(x.shape[1] // BLOCK):
        for part, half in enumerate((hi, hi, lo)):
            at = lane + (3 * k + part) * BLOCK
            ref[rows, at : at + BLOCK] = half[:, k * BLOCK : (k + 1) * BLOCK]


def right_form(ref, row, x):
    hi, lo = split(x)
    for k in range(x.shape[0] // BLOCK):
        for part, half in enumerate((hi, lo, hi)):
            at = row + (3 * k + part) * BLOCK
            ref[at : at + BLOCK, :] = half[k * BLOCK : (k + 1) * BLOCK, :]


def mul(a, b):
    return jnp.dot(a, b, preferred_element_type=f32)


def row_place(at):
    sib, y, core, z, xh = (at[i] for i in range(5))
    return (sib * 4 + y) * 2 + core, z * 2 + xh


def rows_kernel(at, own, up, down, far, far2, inverses, l0, a1, l0_own, inv, raw, left, w0):
    z, xh = at[3], at[4]
    my_row, my_col = row_place(at)
    around = lambda dz, flip: (z + dz + 4) % 4 * 2 + jnp.where(flip, 1 - xh, xh)
    pieces = [
        (own, 0, around(0, False)),
        (own, 8, around(0, True)),
        (up, 0, around(-1, False)),
        (up, 8, around(-1, True)),
        (down, 0, around(1, False)),
        (down, 8, around(1, True)),
        (far, 0, around(2, False)),
        (far2, 0, around(2, True)),
    ]
    for piece, first, source in pieces:
        lanes = pl.ds(pl.multiple_of(source % PT * TILE, TILE), TILE)

        @pl.when(source < PT)
        def _():
            for a in range(LROWS):
                raw[a * TILE : (a + 1) * TILE, lanes] = piece[first + a]

        @pl.when(source >= PT)
        def _():
            for a in range(LROWS):
                a1[a * TILE : (a + 1) * TILE, lanes] = piece[first + a]

    for p in range(NPANEL):
        left_form(inv.at[p], slice(None), 0, inverses[p])
    right_form(w0, 0, inverses[0].T)
    height = 512
    for i in range(LROWS * TILE // height):
        rows = slice(i * height, (i + 1) * height)
        left_form(left, rows, 0, raw[rows, :])
        low = mul(left[rows, : KP // 2], w0[: KP // 2, :BLOCK])
        high = mul(left[rows, :], w0[:, BLOCK:])
        if i == 0:
            tile = jnp.where(
                lax.broadcasted_iota(i32, (height, 1), 0) < TILE, my_row, NF
            )
            low = jnp.where(tile >= PT, low, 0.0)
            high = jnp.where(tile >= PT, high, 0.0)
        raw[rows, :BLOCK] = low
        raw[rows, BLOCK:] = high
        left_form(l0, rows, 0, low)
        left_form(l0, rows, KP // 2, high)
    lanes = pl.ds(pl.multiple_of(my_col % PT * TILE, TILE), TILE)
    for a in range(LROWS):
        l0_own[a] = raw[a * TILE : (a + 1) * TILE, lanes]


def rows_factor(at, pieces, inverses):
    vmem = pl.BlockSpec(memory_space=pltpu.VMEM)
    height = LROWS * TILE
    shapes = [
        ((height, KP), bf16),
        ((height, PANEL), f32),
        ((LROWS, TILE, TILE), f32),
        ((NPANEL, PANEL, KP), bf16),
    ]
    return pl.pallas_call(
        rows_kernel,
        out_shape=[jax.ShapeDtypeStruct(s, t) for s, t in shapes],
        in_specs=[pl.BlockSpec(memory_space=pltpu.SMEM)] + [vmem] * 6,
        out_specs=[vmem] * 4,
        scratch_shapes=[
            pltpu.VMEM((height, PANEL), f32),
            pltpu.VMEM((height, KP), bf16),
            pltpu.VMEM((KP, PANEL), bf16),
        ],
        compiler_params=pltpu.CompilerParams(vmem_limit_bytes=32 * MIB),
        cost_estimate=pl.CostEstimate(
            flops=4_000_000_000, bytes_accessed=14 * MIB, transcendentals=0
        ),
        name="rows_factor",
    )(at, *pieces, inverses)


def update_kernel(
    at, column, corner, front, l0, a1, l0_own, inv, inverses, out, l1, c, raw, right, big, low, low_t, l1_own
):
    step = pl.program_id(0)
    z = at[3]
    my_row, my_col = row_place(at)

    def factor_columns(x, inverse, put):
        put(0, mul(inverse[:BLOCK, : KP // 2], x[: KP // 2, :]))
        put(1, mul(inverse[BLOCK:, :], x[...]))

    @pl.when(step == 0)
    def _():
        for i in range(PT):
            for j in range(PT):
                raw_t = corner[i, j].T
                big[j * TILE : (j + 1) * TILE, i * TILE : (i + 1) * TILE] = raw_t
        right_form(low_t, 0, big[:PANEL, :])

        def put(half, value):
            big[half * BLOCK : (half + 1) * BLOCK, :] = value

        factor_columns(low_t, inv[0], put)
        right_form(low_t, 0, big[:PANEL, :])
        left_form(low, slice(None), 0, big[:PANEL, :].T)
        big[...] = a1[...] - mul(l0[...], low_t[...])
        left_form(l1, slice(None), 0, big[...])
        right_form(low_t, 0, inverses[1].T)
        tile = jnp.where(
            lax.broadcasted_iota(i32, (LROWS * TILE, 1), 0) < TILE, my_row, NF
        )
        first = mul(l1[:, : KP // 2], low_t[: KP // 2, :BLOCK])
        second = mul(l1[...], low_t[:, BLOCK:])
        first = jnp.where(tile >= 2 * PT, first, 0.0)
        second = jnp.where(tile >= 2 * PT, second, 0.0)
        big[:, :BLOCK] = first
        big[:, BLOCK:] = second
        left_form(l1, slice(None), 0, first)
        left_form(l1, slice(None), KP // 2, second)
        lanes = pl.ds(pl.multiple_of(my_col % PT * TILE, TILE), TILE)
        for t in range(LROWS):
            l1_own[t] = big[t * TILE : (t + 1) * TILE, lanes]

    for s in range(2):
        for py in range(4):
            for pc in range(2):
                source = (py - z + 4) % 4 * 2 + pc
                rows = pl.ds(pl.multiple_of(source * TILE, TILE), TILE)
                tile_t = column[(s * 4 + py) * 2 + pc, 0].T
                raw[rows, s * TILE : (s + 1) * TILE] = tile_t
    col_tile = jnp.where(
        (step == 0) & (lax.broadcasted_iota(i32, (1, 2 * TILE), 1) < TILE), my_col, NF
    )
    right_form(right, 0, raw[:PANEL, :])

    def put(panel):
        def store(half, value):
            value = jnp.where(col_tile >= (panel + 1) * PT, value, 0.0)
            right_form(c, panel * KP + half * KP // 2, value)

        return store

    factor_columns(right, inv[0], put(0))
    right_form(right, 0, raw[PANEL:, :] - mul(low[...], c[:KP, :]))
    factor_columns(right, inv[1], put(1))

    change = mul(l0[...], c[:KP, :]) + mul(l1[...], c[KP:, :])
    for t in range(LROWS):
        for b in range(2):
            piece = change[t * TILE : (t + 1) * TILE, b * TILE : (b + 1) * TILE]
            out[t, b] = front[t, b] - piece

    @pl.when(step == 0)
    def _():
        for own, mine in ((l0_own, my_col < PT), (l1_own, my_col >= PT)):

            @pl.when(mine)
            def _():
                for t in range(1, LROWS):
                    out[t, 0] = own[t]

                @pl.when((my_row >= 2 * PT) | ((my_row >= PT) & (my_col < PT)))
                def _():
                    out[0, 0] = own[0]


def update(at, column, front, l0, a1, l0_own, inv, inverses):
    height = LROWS * TILE
    vmem = pl.BlockSpec(memory_space=pltpu.VMEM)
    block = pl.BlockSpec((LROWS, 2, TILE, TILE), lambda j: (0, j, 0, 0))
    return pl.pallas_call(
        update_kernel,
        grid=(LCOLS // 2,),
        out_shape=jax.ShapeDtypeStruct((LROWS, LCOLS, TILE, TILE), f32),
        in_specs=[
            pl.BlockSpec(memory_space=pltpu.SMEM),
            pl.BlockSpec((16, 1, TILE, TILE), lambda j: (0, j, 0, 0)),
            pl.BlockSpec((PT, PT, TILE, TILE), lambda j: (1, 2, 0, 0)),
            block,
        ]
        + [vmem] * 5,
        out_specs=block,
        scratch_shapes=[
            pltpu.VMEM((height, KP), bf16),
            pltpu.VMEM((2 * KP, 2 * TILE), bf16),
            pltpu.VMEM((WIDE, 2 * TILE), f32),
            pltpu.VMEM((KP, 2 * TILE), bf16),
            pltpu.VMEM((height, PANEL), f32),
            pltpu.VMEM((PANEL, KP), bf16),
            pltpu.VMEM((KP, PANEL), bf16),
            pltpu.VMEM((LROWS, TILE, TILE), f32),
        ],
        compiler_params=pltpu.CompilerParams(vmem_limit_bytes=40 * MIB),
        cost_estimate=pl.CostEstimate(
            flops=24_000_000_000, bytes_accessed=30 * MIB, transcendentals=0
        ),
        name="update",
    )(at, column, column, front, l0, a1, l0_own, inv, inverses)


def move(x, axis, size, to):
    return lax.ppermute(x, axis, [(i, to(i)) for i in range(size)])


def gather_row(x):
    up, down = lambda c: (c + 2) % 8, lambda c: (c - 2) % 8
    own = jnp.concatenate([x, move(x, "col", 8, lambda c: c ^ 1)], axis=0)
    from_up, from_down = move(own, "col", 8, up), move(own, "col", 8, down)
    far = move(from_up[:LROWS], "col", 8, up)
    far2 = move(from_down[LROWS:], "col", 8, down)
    return [own, from_up, from_down, far, far2]


def gather_column(x):
    moves = []
    for y in range(4):
        for core in range(2):
            for z in range(4):
                for xh in range(2):
                    to = ((y + z) % 4 * 2 + xh) * 8 + y * 2 + core
                    moves.append(((y * 2 + core) * 8 + z * 2 + xh, to))
    there = lax.ppermute(x, ("row", "col"), moves)
    top = jnp.broadcast_to(x[:1], (8, TILE, TILE))
    top = lax.all_to_all(top, "col", split_axis=0, concat_axis=0, tiled=True)[:PT]
    return lax.all_gather(jnp.concatenate([there, top], axis=0), ("sib", "row"))


def local(child_tiles, child_rows, child_slots, tile_count, inverses):
    grid_rows = lax.axis_size("sib") * lax.axis_size("row")
    columns = lax.axis_size("col")
    devices = grid_rows * columns
    slot_ids = child_slots[0, 0]
    live = tile_count[0]
    row_list = child_rows[0]
    child_row, child_col = slot_ids // CHILD_TILES, slot_ids % CHILD_TILES
    positions = jnp.arange(CHILD_TILES, dtype=i32)
    lookup = lambda x: jnp.sum(
        jnp.where(x[:, None] == positions[None, :], row_list[None, :], 0), axis=1
    )
    parent_row, parent_col = lookup(child_row), lookup(child_col)
    owner = parent_row % grid_rows * columns + parent_col % columns
    target = parent_row // grid_rows * LCOLS + parent_col // columns
    order = jnp.arange(slot_ids.shape[0], dtype=i32)
    is_live = order < live
    earlier = (
        (owner[:, None] == owner[None, :])
        & is_live[None, :]
        & (order[None, :] < order[:, None])
    )
    rank = jnp.sum(earlier.astype(i32), axis=1)
    place = jnp.where(is_live, owner * CAP + rank, devices * CAP)
    filled = place[None, :] == jnp.arange(devices * CAP, dtype=i32)[:, None]
    destined = jnp.sum(jnp.where(filled, target[None, :] + 1, 0), axis=1)
    me = lax.axis_index(("sib", "row", "col"))
    mine = jnp.arange(devices, dtype=i32) == me
    meta = jnp.where(mine, destined.reshape(devices, CAP, 1), 0).astype(f32)
    meta = jnp.pad(meta, ((0, 0), (0, META - CAP), (0, 0)))
    outgoing = pack(place, live, child_tiles[0, 0], meta)
    arrived = lax.all_to_all(
        outgoing, ("sib", "row", "col"), split_axis=0, concat_axis=0, tiled=True
    )
    panel, landing = add_up(True, arrived)
    column = gather_column(panel)
    pieces = gather_row(panel)
    row = lax.axis_index("row")
    col = lax.axis_index("col")
    at = jnp.stack([lax.axis_index("sib"), row // 2, row % 2, col // 2, col % 2])
    at = at.astype(i32)
    front = add_up(False, arrived, landing)
    l0, a1, l0_own, inv = rows_factor(at, pieces, inverses)
    out = update(at, column, front, l0, a1, l0_own, inv, inverses)
    return out.reshape(LROWS, 1, LCOLS, 1, TILE, TILE)


def solution(mesh):
    return jax.shard_map(
        local,
        mesh=mesh,
        in_specs=(
            P("sib", ("row", "col"), None, None, None),
            P("sib", None),
            P("sib", ("row", "col"), None),
            P("sib", ("row", "col")),
            P(),
        ),
        out_specs=P(None, ("sib", "row"), None, "col", None, None),
        check_vma=False,
    )
```

```python
import functools

import jax
import jax.numpy as jnp
from jax import lax
from jax.experimental import pallas as pl
from jax.experimental.pallas import tpu as pltpu
from jax.sharding import PartitionSpec as P

NF = 16384
TILE = 128
PANEL = 512
NPANEL = 2
CHILD_TILES = 64
CAP = 2
PT = PANEL // TILE
WIDE = NPANEL * PANEL
META = 8
LROWS, LCOLS = 8, 16
f32, bf16, i32 = jnp.float32, jnp.bfloat16, jnp.int32
MIB = 1 << 20


def split(x):
    hi = x.astype(bf16)
    return hi, (x - hi.astype(f32)).astype(bf16)


def pack_kernel(place, live, tiles, meta, out, sem, meta_sem):
    head = pltpu.make_async_copy(meta, out.at[:, CAP * TILE :, :], meta_sem)
    head.start()

    def copy(m):
        d = place[m] // CAP
        k = place[m] % CAP
        return pltpu.make_async_copy(
            tiles.at[m], out.at[d, pl.ds(pl.multiple_of(k * TILE, TILE), TILE), :], sem
        )

    lax.fori_loop(0, live[0], lambda m, c: (copy(m).start(), c)[1], 0)
    lax.fori_loop(0, live[0], lambda m, c: (copy(m).wait(), c)[1], 0)
    head.wait()


def pack(place, live, tiles, meta):
    devices = meta.shape[0]
    return pl.pallas_call(
        pack_kernel,
        out_shape=jax.ShapeDtypeStruct((devices, CAP * TILE + META, TILE), f32),
        in_specs=[
            pl.BlockSpec(memory_space=pltpu.SMEM),
            pl.BlockSpec(memory_space=pltpu.SMEM),
            pl.BlockSpec(memory_space=pl.ANY),
            pl.BlockSpec(memory_space=pltpu.VMEM),
        ],
        out_specs=pl.BlockSpec(memory_space=pl.ANY),
        scratch_shapes=[pltpu.SemaphoreType.DMA, pltpu.SemaphoreType.DMA],
        compiler_params=pltpu.CompilerParams(vmem_limit_bytes=60 * MIB),
        name="pack",
    )(place, live, tiles, meta)


def add_kernel(panel, *refs):
    if panel:
        arrived, out, landing, buf, where_to, sem, head, places, head_sem = refs
        slots = arrived.shape[0] * CAP
        copy = pltpu.make_async_copy(arrived.at[:, CAP * TILE :, :], head, head_sem)
        copy.start()
        copy.wait()
        places[...] = jnp.sum(head[...], axis=0).astype(i32) - 1
        copy = pltpu.make_async_copy(places, landing, head_sem)
        copy.start()
        out[...] = jnp.zeros_like(out)
        copy.wait()
    else:
        landing, arrived, out, buf, where_to, sem = refs
        slots = arrived.shape[0] * CAP

    def fetch(k, n):
        pair, turn = k // CAP, k % CAP
        rows = pl.ds(pl.multiple_of(turn * TILE, TILE), TILE)
        return pltpu.make_async_copy(arrived.at[pair, rows, :], buf.at[n], sem)

    def scan(k, n):
        t = landing[k % CAP, k // CAP]
        hit = (t >= 0) & (t % LCOLS == 0) if panel else t >= 0

        @pl.when(hit)
        def _():
            where_to[n] = t
            fetch(k, n).start()

        return n + hit.astype(i32)

    count = lax.fori_loop(0, slots, scan, 0)
    if not panel:
        out[...] = jnp.zeros_like(out)
    lax.fori_loop(0, count, lambda n, c: (fetch(0, n).wait(), c)[1], 0)

    def add(n, c):
        t = where_to[n]
        if panel:
            a = t // LCOLS
            out[a] = out[a] + buf[n]
        else:
            a, b = t // LCOLS, t % LCOLS
            out[a, b] = out[a, b] + buf[n]
        return c

    lax.fori_loop(0, count, add, 0)


def add_up(panel, arrived, landing=None):
    devices = arrived.shape[0]
    vmem = pl.BlockSpec(memory_space=pltpu.VMEM)
    smem = pl.BlockSpec(memory_space=pltpu.SMEM)
    scratch = [
        pltpu.VMEM((devices * CAP, TILE, TILE), f32),
        pltpu.SMEM((devices * CAP,), i32),
        pltpu.SemaphoreType.DMA,
    ]
    any_space = pl.BlockSpec(memory_space=pl.ANY)
    if panel:
        return pl.pallas_call(
            functools.partial(add_kernel, True),
            out_shape=[
                jax.ShapeDtypeStruct((LROWS, TILE, TILE), f32),
                jax.ShapeDtypeStruct((META, devices), i32),
            ],
            in_specs=[any_space],
            out_specs=[vmem, smem],
            scratch_shapes=scratch
            + [
                pltpu.VMEM((devices, META, TILE), f32),
                pltpu.VMEM((META, devices), i32),
                pltpu.SemaphoreType.DMA,
            ],
            compiler_params=pltpu.CompilerParams(vmem_limit_bytes=56 * MIB),
            name="add_panel",
        )(arrived)
    return pl.pallas_call(
        functools.partial(add_kernel, False),
        out_shape=jax.ShapeDtypeStruct((LROWS, LCOLS, TILE, TILE), f32),
        in_specs=[smem, any_space],
        out_specs=vmem,
        scratch_shapes=scratch,
        compiler_params=pltpu.CompilerParams(vmem_limit_bytes=30 * MIB),
        cost_estimate=pl.CostEstimate(
            flops=1000, bytes_accessed=24 * MIB, transcendentals=0
        ),
        name="add_all",
    )(landing, arrived)


BLOCK = 256
KB = 3 * BLOCK
KP = 3 * PANEL


def left_form(ref, lane, x):
    hi, lo = split(x)
    for k in range(x.shape[1] // BLOCK):
        for part, half in enumerate((hi, hi, lo)):
            at = lane + (3 * k + part) * BLOCK
            ref[:, at : at + BLOCK] = half[:, k * BLOCK : (k + 1) * BLOCK]


def right_rows(ref, x):
    hi, lo = split(x)
    for k in range(x.shape[1] // BLOCK):
        for part, half in enumerate((hi, lo, hi)):
            at = (3 * k + part) * BLOCK
            ref[:, at : at + BLOCK] = half[:, k * BLOCK : (k + 1) * BLOCK]


def right_columns(ref, x):
    hi, lo = split(x)
    for k in range(x.shape[0] // BLOCK):
        for part, half in enumerate((hi, lo, hi)):
            at = (3 * k + part) * BLOCK
            ref[at : at + BLOCK, :] = half[k * BLOCK : (k + 1) * BLOCK, :]


def times(a, b):
    return jnp.dot(a, b, preferred_element_type=f32)


def times_transposed(a, b):
    return lax.dot_general(a, b, (((1,), (1,)), ((), ())), preferred_element_type=f32)


def inverse_transposed(x, w):
    return times_transposed(x[:, :KB], w[:BLOCK, :KB]), times_transposed(x[...], w[BLOCK:, :])


def inverse(x, w):
    return times(x[...], w[:, :BLOCK]), times(x[:, KB:], w[KB:, BLOCK:])


def row_factors(at, pieces, corner, inverses, z, own, f0, f1, left, r_rows, r_cols, low):
    dz, xh = at[3], at[4]
    row = (at[0] * 4 + at[1]) * 2 + at[2]
    col = dz * 2 + xh
    around = lambda d, other: (dz + d + 4) % 4 * 2 + (1 - xh if other else xh)
    here, up, down, far, far2 = pieces
    for piece, first, source in (
        (here, 0, around(0, False)),
        (here, 8, around(0, True)),
        (up, 0, around(-1, False)),
        (up, 8, around(-1, True)),
        (down, 0, around(1, False)),
        (down, 8, around(1, True)),
        (far, 0, around(2, False)),
        (far2, 0, around(2, True)),
    ):
        lanes = pl.ds(pl.multiple_of(source % PT * TILE, TILE), TILE)
        for panel, ref in enumerate((f0, f1)):

            @pl.when(source // PT == panel)
            def _():
                for a in range(LROWS):
                    ref[a * TILE : (a + 1) * TILE, lanes] = piece[first + a]

    tile = jnp.where(lax.broadcasted_iota(i32, (LROWS * TILE, 1), 0) < TILE, row, NF)
    my_lanes = pl.ds(pl.multiple_of(col % PT * TILE, TILE), TILE)

    def keep(ref, tiles):
        for a in range(tiles):
            own[a] = ref[a * TILE : (a + 1) * TILE, my_lanes]

    right_rows(r_rows, inverses[0])
    for i in range(PT):
        for j in range(PT):
            low[i * TILE : (i + 1) * TILE, j * TILE : (j + 1) * TILE] = corner[i, j]
    left_form(left.at[:PANEL], 0, low[...])
    one, two = inverse_transposed(left.at[:PANEL], r_rows)
    low[:, :BLOCK] = one
    low[:, BLOCK:] = two
    left_form(left, 0, f0[...])
    one, two = inverse_transposed(left, r_rows)
    f0[:, :BLOCK] = jnp.where(tile >= PT, one, 0.0)
    f0[:, BLOCK:] = jnp.where(tile >= PT, two, 0.0)

    @pl.when(col < PT)
    def _():
        keep(f0, LROWS)

    left_form(left, 0, f0[...])
    right_rows(r_rows, low[...])
    f1[...] = f1[...] - times_transposed(left[...], r_rows[...])

    @pl.when(col >= PT)
    def _():
        keep(f1, 1)

    left_form(left, 0, f1[...])
    right_rows(r_rows, inverses[1])
    one, two = inverse_transposed(left, r_rows)
    f1[:, :BLOCK] = jnp.where(tile >= 2 * PT, one, 0.0)
    f1[:, BLOCK:] = jnp.where(tile >= 2 * PT, two, 0.0)

    @pl.when(col >= PT)
    def _():
        for a in range(1, LROWS):
            own[a] = f1[a * TILE : (a + 1) * TILE, my_lanes]

        @pl.when(row >= 2 * PT)
        def _():
            own[0] = f1[:TILE, my_lanes]

    left_form(left, 0, f1[...])
    right_columns(r_cols, inverses[1])
    one, two = inverse(left, r_cols)
    f1[:, :BLOCK] = one
    f1[:, BLOCK:] = two
    left_form(z, KP, f1[...])
    right_columns(r_cols, low[...])
    f0[...] = f0[...] - times(z[:, KP:], r_cols[...])
    left_form(left, 0, f0[...])
    right_columns(r_cols, inverses[0])
    one, two = inverse(left, r_cols)
    f0[:, :BLOCK] = one
    f0[:, BLOCK:] = two
    left_form(z, 0, f0[...])


def update_kernel(
    at, column, corner, front, here, up, down, far, far2, inverses, out,
    z, right, raw, own, f0, f1, left, r_rows, r_cols, low,
):
    step = pl.program_id(0)

    @pl.when(step == 0)
    def _():
        pieces = here, up, down, far, far2
        row_factors(
            at, pieces, corner, inverses, z, own, f0, f1, left, r_rows, r_cols, low
        )

    for s in range(2):
        for py in range(4):
            for pc in range(2):
                source = (py - at[3] + 4) % 4 * 2 + pc
                lanes = pl.ds(pl.multiple_of(source * TILE, TILE), TILE)
                raw[s * TILE : (s + 1) * TILE, lanes] = column[(s * 4 + py) * 2 + pc, 0]
    right_rows(right, raw[...])
    change = times_transposed(z[...], right[...])
    for t in range(LROWS):
        for b in range(2):
            piece = change[t * TILE : (t + 1) * TILE, b * TILE : (b + 1) * TILE]
            out[t, b] = front[t, b] - piece

    @pl.when(step == 0)
    def _():
        for t in range(1, LROWS):
            out[t, 0] = own[t]

        @pl.when((at[0] * 4 + at[1]) * 2 + at[2] >= PT)
        def _():
            out[0, 0] = own[0]


def update(at, column, front, pieces, inverses):
    height = LROWS * TILE
    vmem = pl.BlockSpec(memory_space=pltpu.VMEM)
    block = pl.BlockSpec((LROWS, 2, TILE, TILE), lambda j: (0, j, 0, 0))
    return pl.pallas_call(
        update_kernel,
        grid=(LCOLS // 2,),
        out_shape=jax.ShapeDtypeStruct((LROWS, LCOLS, TILE, TILE), f32),
        in_specs=[
            pl.BlockSpec(memory_space=pltpu.SMEM),
            pl.BlockSpec((16, 1, TILE, TILE), lambda j: (0, j, 0, 0)),
            pl.BlockSpec((PT, PT, TILE, TILE), lambda j: (1, 2, 0, 0)),
            block,
        ]
        + [vmem] * 6,
        out_specs=block,
        scratch_shapes=[
            pltpu.VMEM((height, 2 * KP), bf16),
            pltpu.VMEM((2 * TILE, 2 * KP), bf16),
            pltpu.VMEM((2 * TILE, WIDE), f32),
            pltpu.VMEM((LROWS, TILE, TILE), f32),
            pltpu.VMEM((height, PANEL), f32),
            pltpu.VMEM((height, PANEL), f32),
            pltpu.VMEM((height, KP), bf16),
            pltpu.VMEM((PANEL, KP), bf16),
            pltpu.VMEM((KP, PANEL), bf16),
            pltpu.VMEM((PANEL, PANEL), f32),
        ],
        compiler_params=pltpu.CompilerParams(vmem_limit_bytes=40 * MIB),
        cost_estimate=pl.CostEstimate(
            flops=24_000_000_000, bytes_accessed=30 * MIB, transcendentals=0
        ),
        name="update",
    )(at, column, column, front, *pieces, inverses)


def move(x, axis, size, to):
    return lax.ppermute(x, axis, [(i, to(i)) for i in range(size)])


def gather_row(x):
    up, down = lambda c: (c + 2) % 8, lambda c: (c - 2) % 8
    own = jnp.concatenate([x, move(x, "col", 8, lambda c: c ^ 1)], axis=0)
    from_up, from_down = move(own, "col", 8, up), move(own, "col", 8, down)
    far = move(from_up[:LROWS], "col", 8, up)
    far2 = move(from_down[LROWS:], "col", 8, down)
    return [own, from_up, from_down, far, far2]


def gather_column(x):
    moves = []
    for y in range(4):
        for core in range(2):
            for z in range(4):
                for xh in range(2):
                    to = ((y + z) % 4 * 2 + xh) * 8 + y * 2 + core
                    moves.append(((y * 2 + core) * 8 + z * 2 + xh, to))
    there = lax.ppermute(x, ("row", "col"), moves)
    top = jnp.broadcast_to(x[:1], (8, TILE, TILE))
    top = lax.all_to_all(top, "col", split_axis=0, concat_axis=0, tiled=True)[:PT]
    return lax.all_gather(jnp.concatenate([there, top], axis=0), ("sib", "row"))


def local(child_tiles, child_rows, child_slots, tile_count, inverses):
    grid_rows = lax.axis_size("sib") * lax.axis_size("row")
    columns = lax.axis_size("col")
    devices = grid_rows * columns
    slot_ids = child_slots[0, 0]
    live = tile_count[0]
    row_list = child_rows[0]
    child_row, child_col = slot_ids // CHILD_TILES, slot_ids % CHILD_TILES
    positions = jnp.arange(CHILD_TILES, dtype=i32)
    lookup = lambda x: jnp.sum(
        jnp.where(x[:, None] == positions[None, :], row_list[None, :], 0), axis=1
    )
    parent_row, parent_col = lookup(child_row), lookup(child_col)
    owner = parent_row % grid_rows * columns + parent_col % columns
    target = parent_row // grid_rows * LCOLS + parent_col // columns
    order = jnp.arange(slot_ids.shape[0], dtype=i32)
    is_live = order < live
    earlier = (
        (owner[:, None] == owner[None, :])
        & is_live[None, :]
        & (order[None, :] < order[:, None])
    )
    rank = jnp.sum(earlier.astype(i32), axis=1)
    place = jnp.where(is_live, owner * CAP + rank, devices * CAP)
    filled = place[None, :] == jnp.arange(devices * CAP, dtype=i32)[:, None]
    destined = jnp.sum(jnp.where(filled, target[None, :] + 1, 0), axis=1)
    me = lax.axis_index(("sib", "row", "col"))
    mine = jnp.arange(devices, dtype=i32) == me
    meta = jnp.where(mine, destined.reshape(devices, CAP, 1), 0).astype(f32)
    meta = jnp.pad(meta, ((0, 0), (0, META - CAP), (0, 0)))
    outgoing = pack(place, live, child_tiles[0, 0], meta)
    arrived = lax.all_to_all(
        outgoing, ("sib", "row", "col"), split_axis=0, concat_axis=0, tiled=True
    )
    panel, landing = add_up(True, arrived)
    column = gather_column(panel)
    pieces = gather_row(panel)
    row = lax.axis_index("row")
    col = lax.axis_index("col")
    at = jnp.stack([lax.axis_index("sib"), row // 2, row % 2, col // 2, col % 2])
    at = at.astype(i32)
    front = add_up(False, arrived, landing)
    out = update(at, column, front, pieces, inverses)
    return out.reshape(LROWS, 1, LCOLS, 1, TILE, TILE)


def solution(mesh):
    return jax.shard_map(
        local,
        mesh=mesh,
        in_specs=(
            P("sib", ("row", "col"), None, None, None),
            P("sib", None),
            P("sib", ("row", "col"), None),
            P("sib", ("row", "col")),
            P(),
        ),
        out_specs=P(None, ("sib", "row"), None, "col", None, None),
        check_vma=False,
    )
```

```python
import functools

import jax
import jax.numpy as jnp
from jax import lax
from jax.experimental import pallas as pl
from jax.experimental.pallas import tpu as pltpu
from jax.sharding import PartitionSpec as P

NF = 16384
TILE = 128
PANEL = 512
NPANEL = 2
CHILD_TILES = 64
CAP = 2
PT = PANEL // TILE
WIDE = NPANEL * PANEL
META = 8
LROWS, LCOLS = 8, 16
f32, bf16, i32 = jnp.float32, jnp.bfloat16, jnp.int32
MIB = 1 << 20


def split(x):
    hi = x.astype(bf16)
    return hi, (x - hi.astype(f32)).astype(bf16)


def pack_kernel(place, live, tiles, meta, out, sem):
    def copy(m):
        d = place[m] // CAP
        k = place[m] % CAP
        return pltpu.make_async_copy(
            tiles.at[m], out.at[d, pl.ds(pl.multiple_of(k * TILE, TILE), TILE), :], sem
        )

    lax.fori_loop(0, live[0], lambda m, c: (copy(m).start(), c)[1], 0)
    out[:, CAP * TILE :, :] = meta[...]
    lax.fori_loop(0, live[0], lambda m, c: (copy(m).wait(), c)[1], 0)


def pack(place, live, tiles, meta):
    devices = meta.shape[0]
    return pl.pallas_call(
        pack_kernel,
        out_shape=jax.ShapeDtypeStruct((devices, CAP * TILE + META, TILE), f32),
        in_specs=[
            pl.BlockSpec(memory_space=pltpu.SMEM),
            pl.BlockSpec(memory_space=pltpu.SMEM),
            pl.BlockSpec(memory_space=pltpu.HBM),
            pl.BlockSpec(memory_space=pltpu.VMEM),
        ],
        out_specs=pl.BlockSpec(memory_space=pltpu.VMEM),
        scratch_shapes=[pltpu.SemaphoreType.DMA],
        compiler_params=pltpu.CompilerParams(vmem_limit_bytes=24 * MIB),
        name="pack",
    )(place, live, tiles, meta)


def add_kernel(panel, *refs):
    if panel:
        arrived, out, landing, buf, where_to, sem, head, places, head_sem = refs
        slots = arrived.shape[0] * CAP
        copy = pltpu.make_async_copy(arrived.at[:, CAP * TILE :, :], head, head_sem)
        copy.start()
        copy.wait()
        places[...] = jnp.sum(head[...], axis=0).astype(i32) - 1
        copy = pltpu.make_async_copy(places, landing, head_sem)
        copy.start()
        out[...] = jnp.zeros_like(out)
        copy.wait()
    else:
        landing, arrived, out, buf, where_to, sem = refs
        slots = arrived.shape[0] * CAP

    def fetch(k, n):
        pair, turn = k // CAP, k % CAP
        rows = pl.ds(pl.multiple_of(turn * TILE, TILE), TILE)
        return pltpu.make_async_copy(arrived.at[pair, rows, :], buf.at[n], sem)

    def scan(k, n):
        t = landing[k % CAP, k // CAP]
        hit = (t >= 0) & (t % LCOLS == 0) if panel else t >= 0

        @pl.when(hit)
        def _():
            where_to[n] = t
            fetch(k, n).start()

        return n + hit.astype(i32)

    count = lax.fori_loop(0, slots, scan, 0)
    if not panel:
        out[...] = jnp.zeros_like(out)
    lax.fori_loop(0, count, lambda n, c: (fetch(0, n).wait(), c)[1], 0)

    def add(n, c):
        t = where_to[n]
        if panel:
            a = t // LCOLS
            out[a] = out[a] + buf[n]
        else:
            a, b = t // LCOLS, t % LCOLS
            out[a, b] = out[a, b] + buf[n]
        return c

    lax.fori_loop(0, count, add, 0)


def add_up(panel, arrived, landing=None):
    devices = arrived.shape[0]
    vmem = pl.BlockSpec(memory_space=pltpu.VMEM)
    smem = pl.BlockSpec(memory_space=pltpu.SMEM)
    scratch = [
        pltpu.VMEM((devices * CAP, TILE, TILE), f32),
        pltpu.SMEM((devices * CAP,), i32),
        pltpu.SemaphoreType.DMA,
    ]
    any_space = pl.BlockSpec(memory_space=pl.ANY)
    if panel:
        return pl.pallas_call(
            functools.partial(add_kernel, True),
            out_shape=[
                jax.ShapeDtypeStruct((LROWS, TILE, TILE), f32),
                jax.ShapeDtypeStruct((META, devices), i32),
            ],
            in_specs=[any_space],
            out_specs=[vmem, smem],
            scratch_shapes=scratch
            + [
                pltpu.VMEM((devices, META, TILE), f32),
                pltpu.VMEM((META, devices), i32),
                pltpu.SemaphoreType.DMA,
            ],
            compiler_params=pltpu.CompilerParams(vmem_limit_bytes=56 * MIB),
            name="add_panel",
        )(arrived)
    return pl.pallas_call(
        functools.partial(add_kernel, False),
        out_shape=jax.ShapeDtypeStruct((LROWS, LCOLS, TILE, TILE), f32),
        in_specs=[smem, any_space],
        out_specs=vmem,
        scratch_shapes=scratch,
        compiler_params=pltpu.CompilerParams(vmem_limit_bytes=30 * MIB),
        cost_estimate=pl.CostEstimate(
            flops=1000, bytes_accessed=24 * MIB, transcendentals=0
        ),
        name="add_all",
    )(landing, arrived)


BLOCK = 256
KB = 3 * BLOCK
KP = 3 * PANEL


def left_form(ref, lane, x):
    hi, lo = split(x)
    for k in range(x.shape[1] // BLOCK):
        for part, half in enumerate((hi, hi, lo)):
            at = lane + (3 * k + part) * BLOCK
            ref[:, at : at + BLOCK] = half[:, k * BLOCK : (k + 1) * BLOCK]


def right_rows(ref, x):
    hi, lo = split(x)
    for k in range(x.shape[1] // BLOCK):
        for part, half in enumerate((hi, lo, hi)):
            at = (3 * k + part) * BLOCK
            ref[:, at : at + BLOCK] = half[:, k * BLOCK : (k + 1) * BLOCK]


def right_columns(ref, x):
    hi, lo = split(x)
    for k in range(x.shape[0] // BLOCK):
        for part, half in enumerate((hi, lo, hi)):
            at = (3 * k + part) * BLOCK
            ref[at : at + BLOCK, :] = half[k * BLOCK : (k + 1) * BLOCK, :]


def times(a, b):
    return jnp.dot(a, b, preferred_element_type=f32)


def times_transposed(a, b):
    return lax.dot_general(a, b, (((1,), (1,)), ((), ())), preferred_element_type=f32)


def inverse_transposed(x, w):
    return times_transposed(x[:, :KB], w[:BLOCK, :KB]), times_transposed(x[...], w[BLOCK:, :])


def inverse(x, w):
    return times(x[...], w[:, :BLOCK]), times(x[:, KB:], w[KB:, BLOCK:])


def row_factors(at, pieces, corner, inverses, z, own, f0, f1, left, r_rows, r_cols, low):
    dz, xh = at[3], at[4]
    row = (at[0] * 4 + at[1]) * 2 + at[2]
    col = dz * 2 + xh
    around = lambda d, other: (dz + d + 4) % 4 * 2 + (1 - xh if other else xh)
    here, up, down, far, far2 = pieces
    for piece, first, source in (
        (here, 0, around(0, False)),
        (here, 8, around(0, True)),
        (up, 0, around(-1, False)),
        (up, 8, around(-1, True)),
        (down, 0, around(1, False)),
        (down, 8, around(1, True)),
        (far, 0, around(2, False)),
        (far2, 0, around(2, True)),
    ):
        lanes = pl.ds(pl.multiple_of(source % PT * TILE, TILE), TILE)
        for panel, ref in enumerate((f0, f1)):

            @pl.when(source // PT == panel)
            def _():
                for a in range(LROWS):
                    ref[a * TILE : (a + 1) * TILE, lanes] = piece[first + a]

    tile = jnp.where(lax.broadcasted_iota(i32, (LROWS * TILE, 1), 0) < TILE, row, NF)
    my_lanes = pl.ds(pl.multiple_of(col % PT * TILE, TILE), TILE)

    def keep(ref, tiles):
        for a in range(tiles):
            own[a] = ref[a * TILE : (a + 1) * TILE, my_lanes]

    right_rows(r_rows, inverses[0])
    for i in range(PT):
        for j in range(PT):
            low[i * TILE : (i + 1) * TILE, j * TILE : (j + 1) * TILE] = corner[i, j]
    left_form(left.at[:PANEL], 0, low[...])
    one, two = inverse_transposed(left.at[:PANEL], r_rows)
    low[:, :BLOCK] = one
    low[:, BLOCK:] = two
    left_form(left, 0, f0[...])
    one, two = inverse_transposed(left, r_rows)
    f0[:, :BLOCK] = jnp.where(tile >= PT, one, 0.0)
    f0[:, BLOCK:] = jnp.where(tile >= PT, two, 0.0)

    @pl.when(col < PT)
    def _():
        keep(f0, LROWS)

    left_form(left, 0, f0[...])
    right_rows(r_rows, low[...])
    f1[...] = f1[...] - times_transposed(left[...], r_rows[...])

    @pl.when(col >= PT)
    def _():
        keep(f1, 1)

    left_form(left, 0, f1[...])
    right_rows(r_rows, inverses[1])
    one, two = inverse_transposed(left, r_rows)
    f1[:, :BLOCK] = jnp.where(tile >= 2 * PT, one, 0.0)
    f1[:, BLOCK:] = jnp.where(tile >= 2 * PT, two, 0.0)

    @pl.when(col >= PT)
    def _():
        for a in range(1, LROWS):
            own[a] = f1[a * TILE : (a + 1) * TILE, my_lanes]

        @pl.when(row >= 2 * PT)
        def _():
            own[0] = f1[:TILE, my_lanes]

    left_form(left, 0, f1[...])
    right_columns(r_cols, inverses[1])
    one, two = inverse(left, r_cols)
    f1[:, :BLOCK] = one
    f1[:, BLOCK:] = two
    left_form(z, KP, f1[...])
    right_columns(r_cols, low[...])
    f0[...] = f0[...] - times(z[:, KP:], r_cols[...])
    left_form(left, 0, f0[...])
    right_columns(r_cols, inverses[0])
    one, two = inverse(left, r_cols)
    f0[:, :BLOCK] = one
    f0[:, BLOCK:] = two
    left_form(z, 0, f0[...])


def update_kernel(
    at, column, corner, front, here, up, down, far, far2, inverses, out,
    z, right, raw, own, f0, f1, left, r_rows, r_cols, low,
):
    step = pl.program_id(0)

    @pl.when(step == 0)
    def _():
        pieces = here, up, down, far, far2
        row_factors(
            at, pieces, corner, inverses, z, own, f0, f1, left, r_rows, r_cols, low
        )

    for s in range(2):
        for py in range(4):
            for pc in range(2):
                source = (py - at[3] + 4) % 4 * 2 + pc
                lanes = pl.ds(pl.multiple_of(source * TILE, TILE), TILE)
                raw[s * TILE : (s + 1) * TILE, lanes] = column[(s * 4 + py) * 2 + pc, 0]
    right_rows(right, raw[...])
    change = times_transposed(z[...], right[...])
    for t in range(LROWS):
        for b in range(2):
            piece = change[t * TILE : (t + 1) * TILE, b * TILE : (b + 1) * TILE]
            out[t, b] = front[t, b] - piece

    @pl.when(step == 0)
    def _():
        for t in range(1, LROWS):
            out[t, 0] = own[t]

        @pl.when((at[0] * 4 + at[1]) * 2 + at[2] >= PT)
        def _():
            out[0, 0] = own[0]


def update(at, column, front, pieces, inverses):
    height = LROWS * TILE
    vmem = pl.BlockSpec(memory_space=pltpu.VMEM)
    block = pl.BlockSpec((LROWS, 2, TILE, TILE), lambda j: (0, j, 0, 0))
    return pl.pallas_call(
        update_kernel,
        grid=(LCOLS // 2,),
        out_shape=jax.ShapeDtypeStruct((LROWS, LCOLS, TILE, TILE), f32),
        in_specs=[
            pl.BlockSpec(memory_space=pltpu.SMEM),
            pl.BlockSpec((16, 1, TILE, TILE), lambda j: (0, j, 0, 0)),
            pl.BlockSpec((PT, PT, TILE, TILE), lambda j: (1, 2, 0, 0)),
            block,
        ]
        + [vmem] * 6,
        out_specs=block,
        scratch_shapes=[
            pltpu.VMEM((height, 2 * KP), bf16),
            pltpu.VMEM((2 * TILE, 2 * KP), bf16),
            pltpu.VMEM((2 * TILE, WIDE), f32),
            pltpu.VMEM((LROWS, TILE, TILE), f32),
            pltpu.VMEM((height, PANEL), f32),
            pltpu.VMEM((height, PANEL), f32),
            pltpu.VMEM((height, KP), bf16),
            pltpu.VMEM((PANEL, KP), bf16),
            pltpu.VMEM((KP, PANEL), bf16),
            pltpu.VMEM((PANEL, PANEL), f32),
        ],
        compiler_params=pltpu.CompilerParams(vmem_limit_bytes=40 * MIB),
        cost_estimate=pl.CostEstimate(
            flops=24_000_000_000, bytes_accessed=30 * MIB, transcendentals=0
        ),
        name="update",
    )(at, column, column, front, *pieces, inverses)


def move(x, axis, size, to):
    return lax.ppermute(x, axis, [(i, to(i)) for i in range(size)])


def gather_row(x):
    up, down = lambda c: (c + 2) % 8, lambda c: (c - 2) % 8
    own = jnp.concatenate([x, move(x, "col", 8, lambda c: c ^ 1)], axis=0)
    from_up, from_down = move(own, "col", 8, up), move(own, "col", 8, down)
    far = move(from_up[:LROWS], "col", 8, up)
    far2 = move(from_down[LROWS:], "col", 8, down)
    return [own, from_up, from_down, far, far2]


def gather_column(x):
    moves = []
    for y in range(4):
        for core in range(2):
            for z in range(4):
                for xh in range(2):
                    to = ((y + z) % 4 * 2 + xh) * 8 + y * 2 + core
                    moves.append(((y * 2 + core) * 8 + z * 2 + xh, to))
    there = lax.ppermute(x, ("row", "col"), moves)
    top = jnp.broadcast_to(x[:1], (8, TILE, TILE))
    top = lax.all_to_all(top, "col", split_axis=0, concat_axis=0, tiled=True)[:PT]
    return lax.all_gather(jnp.concatenate([there, top], axis=0), ("sib", "row"))


def local(child_tiles, child_rows, child_slots, tile_count, inverses):
    grid_rows = lax.axis_size("sib") * lax.axis_size("row")
    columns = lax.axis_size("col")
    devices = grid_rows * columns
    slot_ids = child_slots[0, 0]
    live = tile_count[0]
    row_list = child_rows[0]
    child_row, child_col = slot_ids // CHILD_TILES, slot_ids % CHILD_TILES
    positions = jnp.arange(CHILD_TILES, dtype=i32)
    lookup = lambda x: jnp.sum(
        jnp.where(x[:, None] == positions[None, :], row_list[None, :], 0), axis=1
    )
    parent_row, parent_col = lookup(child_row), lookup(child_col)
    owner = parent_row % grid_rows * columns + parent_col % columns
    target = parent_row // grid_rows * LCOLS + parent_col // columns
    order = jnp.arange(slot_ids.shape[0], dtype=i32)
    is_live = order < live
    earlier = (
        (owner[:, None] == owner[None, :])
        & is_live[None, :]
        & (order[None, :] < order[:, None])
    )
    rank = jnp.sum(earlier.astype(i32), axis=1)
    place = jnp.where(is_live, owner * CAP + rank, devices * CAP)
    filled = place[None, :] == jnp.arange(devices * CAP, dtype=i32)[:, None]
    destined = jnp.sum(jnp.where(filled, target[None, :] + 1, 0), axis=1)
    me = lax.axis_index(("sib", "row", "col"))
    mine = jnp.arange(devices, dtype=i32) == me
    meta = jnp.where(mine, destined.reshape(devices, CAP, 1), 0).astype(f32)
    meta = jnp.pad(meta, ((0, 0), (0, META - CAP), (0, 0)))
    outgoing = pack(place, live, child_tiles[0, 0], meta)
    arrived = lax.all_to_all(
        outgoing, ("sib", "row", "col"), split_axis=0, concat_axis=0, tiled=True
    )
    panel, landing = add_up(True, arrived)
    column = gather_column(panel)
    pieces = gather_row(panel)
    row = lax.axis_index("row")
    col = lax.axis_index("col")
    at = jnp.stack([lax.axis_index("sib"), row // 2, row % 2, col // 2, col % 2])
    at = at.astype(i32)
    front = add_up(False, arrived, landing)
    out = update(at, column, front, pieces, inverses)
    return out.reshape(LROWS, 1, LCOLS, 1, TILE, TILE)


def solution(mesh):
    return jax.shard_map(
        local,
        mesh=mesh,
        in_specs=(
            P("sib", ("row", "col"), None, None, None),
            P("sib", None),
            P("sib", ("row", "col"), None),
            P("sib", ("row", "col")),
            P(),
        ),
        out_specs=P(None, ("sib", "row"), None, "col", None, None),
        check_vma=False,
    )
```

```python
import functools

import jax
import jax.numpy as jnp
from jax import lax
from jax.experimental import pallas as pl
from jax.experimental.pallas import tpu as pltpu
from jax.sharding import PartitionSpec as P

NF = 16384
TILE = 128
PANEL = 512
NPANEL = 2
CHILD_TILES = 64
CAP = 2
PT = PANEL // TILE
WIDE = NPANEL * PANEL
META = 8
LROWS, LCOLS = 8, 16
f32, bf16, i32 = jnp.float32, jnp.bfloat16, jnp.int32
MIB = 1 << 20


def split(x):
    hi = x.astype(bf16)
    return hi, (x - hi.astype(f32)).astype(bf16)


def pack_kernel(place, live, tiles, meta, out):
    def put(m, carry):
        d = place[m] // CAP
        k = place[m] % CAP
        out[d, pl.ds(pl.multiple_of(k * TILE, TILE), TILE), :] = tiles[m]
        return carry

    out[:, CAP * TILE :, :] = meta[...]
    lax.fori_loop(0, live[0], put, 0)


def pack(place, live, tiles, meta):
    devices = meta.shape[0]
    vmem = pl.BlockSpec(memory_space=pltpu.VMEM)
    smem = pl.BlockSpec(memory_space=pltpu.SMEM)
    return pl.pallas_call(
        pack_kernel,
        out_shape=jax.ShapeDtypeStruct((devices, CAP * TILE + META, TILE), f32),
        in_specs=[smem, smem, vmem, vmem],
        out_specs=vmem,
        compiler_params=pltpu.CompilerParams(vmem_limit_bytes=16 * MIB),
        name="pack",
    )(place, live, tiles, meta)


def add_kernel(panel, *refs):
    if panel:
        arrived, out, landing, buf, where_to, sem, head, places, head_sem = refs
        slots = arrived.shape[0] * CAP
        copy = pltpu.make_async_copy(arrived.at[:, CAP * TILE :, :], head, head_sem)
        copy.start()
        copy.wait()
        places[...] = jnp.sum(head[...], axis=0).astype(i32) - 1
        copy = pltpu.make_async_copy(places, landing, head_sem)
        copy.start()
        out[...] = jnp.zeros_like(out)
        copy.wait()
    else:
        landing, arrived, out, buf, where_to, sem = refs
        slots = arrived.shape[0] * CAP

    def fetch(k, n):
        pair, turn = k // CAP, k % CAP
        rows = pl.ds(pl.multiple_of(turn * TILE, TILE), TILE)
        return pltpu.make_async_copy(arrived.at[pair, rows, :], buf.at[n], sem)

    def scan(k, n):
        t = landing[k % CAP, k // CAP]
        hit = (t >= 0) & (t % LCOLS == 0) if panel else t >= 0

        @pl.when(hit)
        def _():
            where_to[n] = t
            fetch(k, n).start()

        return n + hit.astype(i32)

    count = lax.fori_loop(0, slots, scan, 0)
    if not panel:
        out[...] = jnp.zeros_like(out)
    lax.fori_loop(0, count, lambda n, c: (fetch(0, n).wait(), c)[1], 0)

    def add(n, c):
        t = where_to[n]
        if panel:
            a = t // LCOLS
            out[a] = out[a] + buf[n]
        else:
            a, b = t // LCOLS, t % LCOLS
            out[a, b] = out[a, b] + buf[n]
        return c

    lax.fori_loop(0, count, add, 0)


def add_up(panel, arrived, landing=None):
    devices = arrived.shape[0]
    vmem = pl.BlockSpec(memory_space=pltpu.VMEM)
    smem = pl.BlockSpec(memory_space=pltpu.SMEM)
    scratch = [
        pltpu.VMEM((devices * CAP, TILE, TILE), f32),
        pltpu.SMEM((devices * CAP,), i32),
        pltpu.SemaphoreType.DMA,
    ]
    any_space = pl.BlockSpec(memory_space=pl.ANY)
    if panel:
        return pl.pallas_call(
            functools.partial(add_kernel, True),
            out_shape=[
                jax.ShapeDtypeStruct((LROWS, TILE, TILE), f32),
                jax.ShapeDtypeStruct((META, devices), i32),
            ],
            in_specs=[any_space],
            out_specs=[vmem, smem],
            scratch_shapes=scratch
            + [
                pltpu.VMEM((devices, META, TILE), f32),
                pltpu.VMEM((META, devices), i32),
                pltpu.SemaphoreType.DMA,
            ],
            compiler_params=pltpu.CompilerParams(vmem_limit_bytes=56 * MIB),
            name="add_panel",
        )(arrived)
    return pl.pallas_call(
        functools.partial(add_kernel, False),
        out_shape=jax.ShapeDtypeStruct((LROWS, LCOLS, TILE, TILE), f32),
        in_specs=[smem, any_space],
        out_specs=vmem,
        scratch_shapes=scratch,
        compiler_params=pltpu.CompilerParams(vmem_limit_bytes=30 * MIB),
        cost_estimate=pl.CostEstimate(
            flops=1000, bytes_accessed=24 * MIB, transcendentals=0
        ),
        name="add_all",
    )(landing, arrived)


BLOCK = 256
KB = 3 * BLOCK
KP = 3 * PANEL


def left_form(ref, lane, x):
    hi, lo = split(x)
    for k in range(x.shape[1] // BLOCK):
        for part, half in enumerate((hi, hi, lo)):
            at = lane + (3 * k + part) * BLOCK
            ref[:, at : at + BLOCK] = half[:, k * BLOCK : (k + 1) * BLOCK]


def right_rows(ref, x):
    hi, lo = split(x)
    for k in range(x.shape[1] // BLOCK):
        for part, half in enumerate((hi, lo, hi)):
            at = (3 * k + part) * BLOCK
            ref[:, at : at + BLOCK] = half[:, k * BLOCK : (k + 1) * BLOCK]


def right_columns(ref, x):
    hi, lo = split(x)
    for k in range(x.shape[0] // BLOCK):
        for part, half in enumerate((hi, lo, hi)):
            at = (3 * k + part) * BLOCK
            ref[at : at + BLOCK, :] = half[k * BLOCK : (k + 1) * BLOCK, :]


def times(a, b):
    return jnp.dot(a, b, preferred_element_type=f32)


def times_transposed(a, b):
    return lax.dot_general(a, b, (((1,), (1,)), ((), ())), preferred_element_type=f32)


def inverse_transposed(x, w):
    return times_transposed(x[:, :KB], w[:BLOCK, :KB]), times_transposed(x[...], w[BLOCK:, :])


def inverse(x, w):
    return times(x[...], w[:, :BLOCK]), times(x[:, KB:], w[KB:, BLOCK:])


def row_factors(at, pieces, corner, inverses, z, own, f0, f1, left, r_rows, r_cols, low):
    dz, xh = at[3], at[4]
    row = (at[0] * 4 + at[1]) * 2 + at[2]
    col = dz * 2 + xh
    around = lambda d, other: (dz + d + 4) % 4 * 2 + (1 - xh if other else xh)
    here, up, down, far, far2 = pieces
    for piece, first, source in (
        (here, 0, around(0, False)),
        (here, 8, around(0, True)),
        (up, 0, around(-1, False)),
        (up, 8, around(-1, True)),
        (down, 0, around(1, False)),
        (down, 8, around(1, True)),
        (far, 0, around(2, False)),
        (far2, 0, around(2, True)),
    ):
        lanes = pl.ds(pl.multiple_of(source % PT * TILE, TILE), TILE)
        for panel, ref in enumerate((f0, f1)):

            @pl.when(source // PT == panel)
            def _():
                for a in range(LROWS):
                    ref[a * TILE : (a + 1) * TILE, lanes] = piece[first + a]

    tile = jnp.where(lax.broadcasted_iota(i32, (LROWS * TILE, 1), 0) < TILE, row, NF)
    my_lanes = pl.ds(pl.multiple_of(col % PT * TILE, TILE), TILE)

    def keep(ref, tiles):
        for a in range(tiles):
            own[a] = ref[a * TILE : (a + 1) * TILE, my_lanes]

    right_rows(r_rows, inverses[0])
    y_bit = jnp.where(at[1] >= 2, at[1], 3 - at[1]) - 2
    for k in range(PT):
        i = (y_bit ^ (k & 1)) * 2 + (at[2] ^ (k >> 1))
        rows = pl.ds(pl.multiple_of(i * TILE, TILE), TILE)
        for j in range(PT):
            here = corner[k >> 1][(k & 1) * PT + j]
            low[rows, j * TILE : (j + 1) * TILE] = here
    left_form(left.at[:PANEL], 0, low[...])
    one, two = inverse_transposed(left.at[:PANEL], r_rows)
    low[:, :BLOCK] = one
    low[:, BLOCK:] = two
    left_form(left, 0, f0[...])
    one, two = inverse_transposed(left, r_rows)
    f0[:, :BLOCK] = jnp.where(tile >= PT, one, 0.0)
    f0[:, BLOCK:] = jnp.where(tile >= PT, two, 0.0)

    @pl.when(col < PT)
    def _():
        keep(f0, LROWS)

    left_form(left, 0, f0[...])
    right_rows(r_rows, low[...])
    f1[...] = f1[...] - times_transposed(left[...], r_rows[...])

    @pl.when(col >= PT)
    def _():
        keep(f1, 1)

    left_form(left, 0, f1[...])
    right_rows(r_rows, inverses[1])
    one, two = inverse_transposed(left, r_rows)
    f1[:, :BLOCK] = jnp.where(tile >= 2 * PT, one, 0.0)
    f1[:, BLOCK:] = jnp.where(tile >= 2 * PT, two, 0.0)

    @pl.when(col >= PT)
    def _():
        for a in range(1, LROWS):
            own[a] = f1[a * TILE : (a + 1) * TILE, my_lanes]

        @pl.when(row >= 2 * PT)
        def _():
            own[0] = f1[:TILE, my_lanes]

    left_form(left, 0, f1[...])
    right_columns(r_cols, inverses[1])
    one, two = inverse(left, r_cols)
    f1[:, :BLOCK] = one
    f1[:, BLOCK:] = two
    left_form(z, KP, f1[...])
    right_columns(r_cols, low[...])
    f0[...] = f0[...] - times(z[:, KP:], r_cols[...])
    left_form(left, 0, f0[...])
    right_columns(r_cols, inverses[0])
    one, two = inverse(left, r_cols)
    f0[:, :BLOCK] = one
    f0[:, BLOCK:] = two
    left_form(z, 0, f0[...])


def update_kernel(
    at, *refs
):
    columns, pieces, corner = refs[:10], refs[10:15], refs[15:17]
    front, inverses, out = refs[17:20]
    z, right, raw, own, f0, f1, left, r_rows, r_cols, low = refs[20:]
    step = pl.program_id(0)

    @pl.when(step == 0)
    def _():
        row_factors(
            at, pieces, corner, inverses, z, own, f0, f1, left, r_rows, r_cols, low
        )

    for k in range(2):
        core = at[2] ^ k
        here, up, down, far, far2 = columns[5 * k : 5 * k + 5]
        for ref, n, other, dy in (
            (here, 0, 0, 0),
            (here, 1, 1, 0),
            (up, 0, 0, -1),
            (up, 1, 1, -1),
            (down, 0, 0, 1),
            (down, 1, 1, 1),
            (far, 0, 0, 2),
            (far2, 0, 1, 2),
        ):
            source = (at[1] + dy - at[3] + 8) % 4 * 2 + core
            rows = pl.ds(pl.multiple_of((at[0] ^ other) * TILE, TILE), TILE)
            lanes = pl.ds(pl.multiple_of(source * TILE, TILE), TILE)
            raw[rows, lanes] = ref[n, 0]
    right_rows(right, raw[...])
    change = times_transposed(z[...], right[...])
    for t in range(LROWS):
        for b in range(2):
            piece = change[t * TILE : (t + 1) * TILE, b * TILE : (b + 1) * TILE]
            out[t, b] = front[t, b] - piece

    @pl.when(step == 0)
    def _():
        for t in range(1, LROWS):
            out[t, 0] = own[t]

        @pl.when((at[0] * 4 + at[1]) * 2 + at[2] >= PT)
        def _():
            out[0, 0] = own[0]


def update(at, columns, front, pieces, corner, inverses):
    height = LROWS * TILE
    vmem = pl.BlockSpec(memory_space=pltpu.VMEM)
    block = pl.BlockSpec((LROWS, 2, TILE, TILE), lambda j: (0, j, 0, 0))
    return pl.pallas_call(
        update_kernel,
        grid=(LCOLS // 2,),
        out_shape=jax.ShapeDtypeStruct((LROWS, LCOLS, TILE, TILE), f32),
        in_specs=[
            pl.BlockSpec(memory_space=pltpu.SMEM),
            *(
                pl.BlockSpec((x.shape[0], 1, TILE, TILE), lambda j: (0, j, 0, 0))
                for x in columns
            ),
            *[vmem] * 7,
            block,
            vmem,
        ],
        out_specs=block,
        scratch_shapes=[
            pltpu.VMEM((height, 2 * KP), bf16),
            pltpu.VMEM((2 * TILE, 2 * KP), bf16),
            pltpu.VMEM((2 * TILE, WIDE), f32),
            pltpu.VMEM((LROWS, TILE, TILE), f32),
            pltpu.VMEM((height, PANEL), f32),
            pltpu.VMEM((height, PANEL), f32),
            pltpu.VMEM((height, KP), bf16),
            pltpu.VMEM((PANEL, KP), bf16),
            pltpu.VMEM((KP, PANEL), bf16),
            pltpu.VMEM((PANEL, PANEL), f32),
        ],
        compiler_params=pltpu.CompilerParams(vmem_limit_bytes=40 * MIB),
        cost_estimate=pl.CostEstimate(
            flops=24_000_000_000, bytes_accessed=30 * MIB, transcendentals=0
        ),
        name="update",
    )(at, *columns, *pieces, *corner, front, inverses)


def move(x, axis, size, to):
    return lax.ppermute(x, axis, [(i, to(i)) for i in range(size)])


def ring_gather(own, axis):
    half = own.shape[0] // 2
    up, down = lambda i: (i + 2) % 8, lambda i: (i - 2) % 8
    before, behind = move(own, axis, 8, up), move(own, axis, 8, down)
    return [own, before, behind, move(before[:half], axis, 8, up), move(behind[half:], axis, 8, down)]


def gather_corner(top):
    sib, row = lax.axis_index("sib"), lax.axis_index("row")
    flip = [(4, 2), (5, 3), (6, 0), (7, 1)]
    a = lax.ppermute(top, "sib", [(0, 1)])
    b = lax.ppermute(top, "row", flip)
    c = lax.ppermute(top, ("sib", "row"), [(i, 8 + j) for i, j in flip])
    mine = jnp.where(row >= 4, jnp.where(sib == 0, top, a), jnp.where(sib == 0, b, c))
    both = jnp.concatenate([mine, move(mine, "row", 8, lambda i: i ^ 2)], axis=0)
    return [both, move(both, "row", 8, lambda i: i ^ 1)]


def gather(panel):
    there = []
    for y in range(4):
        for core in range(2):
            for z in range(4):
                for xh in range(2):
                    to = ((y + z) % 4 * 2 + xh) * 8 + y * 2 + core
                    there.append(((y * 2 + core) * 8 + z * 2 + xh, to))
    across = lax.ppermute(panel, ("row", "col"), there)
    pair = jnp.concatenate([panel, move(panel, "col", 8, lambda i: i ^ 1)], axis=0)
    top = jnp.broadcast_to(panel[:1], (8, TILE, TILE))
    top = lax.all_to_all(top, "col", split_axis=0, concat_axis=0, tiled=True)[:PT]
    pair, top, across = lax.optimization_barrier((pair, top, across))
    pieces = ring_gather(pair, "col")
    corner = gather_corner(top)
    pair = jnp.concatenate([across, move(across, "sib", 2, lambda i: 1 - i)], axis=0)
    columns = ring_gather(pair, "row")
    columns = columns + [move(x, "row", 8, lambda i: i ^ 1) for x in columns]
    columns = [x.reshape(-1, LROWS, TILE, TILE) for x in columns]
    return columns, pieces, corner


def local(child_tiles, child_rows, child_slots, tile_count, inverses):
    grid_rows = lax.axis_size("sib") * lax.axis_size("row")
    columns = lax.axis_size("col")
    devices = grid_rows * columns
    slot_ids = child_slots[0, 0]
    live = tile_count[0]
    row_list = child_rows[0]
    child_row, child_col = slot_ids // CHILD_TILES, slot_ids % CHILD_TILES
    positions = jnp.arange(CHILD_TILES, dtype=i32)
    lookup = lambda x: jnp.sum(
        jnp.where(x[:, None] == positions[None, :], row_list[None, :], 0), axis=1
    )
    parent_row, parent_col = lookup(child_row), lookup(child_col)
    owner = parent_row % grid_rows * columns + parent_col % columns
    target = parent_row // grid_rows * LCOLS + parent_col // columns
    order = jnp.arange(slot_ids.shape[0], dtype=i32)
    is_live = order < live
    earlier = (
        (owner[:, None] == owner[None, :])
        & is_live[None, :]
        & (order[None, :] < order[:, None])
    )
    rank = jnp.sum(earlier.astype(i32), axis=1)
    place = jnp.where(is_live, owner * CAP + rank, devices * CAP)
    filled = place[None, :] == jnp.arange(devices * CAP, dtype=i32)[:, None]
    destined = jnp.sum(jnp.where(filled, target[None, :] + 1, 0), axis=1)
    me = lax.axis_index(("sib", "row", "col"))
    mine = jnp.arange(devices, dtype=i32) == me
    meta = jnp.where(mine, destined.reshape(devices, CAP, 1), 0).astype(f32)
    meta = jnp.pad(meta, ((0, 0), (0, META - CAP), (0, 0)))
    outgoing = pack(place, live, child_tiles[0, 0], meta)
    arrived = lax.all_to_all(
        outgoing, ("sib", "row", "col"), split_axis=0, concat_axis=0, tiled=True
    )
    panel, landing = add_up(True, arrived)
    columns, pieces, corner = gather(panel)
    row = lax.axis_index("row")
    col = lax.axis_index("col")
    at = jnp.stack([lax.axis_index("sib"), row // 2, row % 2, col // 2, col % 2])
    at = at.astype(i32)
    front = add_up(False, arrived, landing)
    out = update(at, columns, front, pieces, corner, inverses)
    return out.reshape(LROWS, 1, LCOLS, 1, TILE, TILE)


def solution(mesh):
    return jax.shard_map(
        local,
        mesh=mesh,
        in_specs=(
            P("sib", ("row", "col"), None, None, None),
            P("sib", None),
            P("sib", ("row", "col"), None),
            P("sib", ("row", "col")),
            P(),
        ),
        out_specs=P(None, ("sib", "row"), None, "col", None, None),
        check_vma=False,
    )
```

```python
import functools

import jax
import jax.numpy as jnp
from jax import lax
from jax.experimental import pallas as pl
from jax.experimental.pallas import tpu as pltpu
from jax.sharding import PartitionSpec as P

NF = 16384
TILE = 128
PANEL = 512
NPANEL = 2
CHILD_TILES = 64
CAP = 2
PT = PANEL // TILE
WIDE = NPANEL * PANEL
META = 8
LROWS, LCOLS = 8, 16
f32, bf16, i32 = jnp.float32, jnp.bfloat16, jnp.int32
MIB = 1 << 20


def split(x):
    hi = x.astype(bf16)
    return hi, (x - hi.astype(f32)).astype(bf16)


def pack_kernel(place, live, tiles, meta, out):
    def put(m, carry):
        d = place[m] // CAP
        k = place[m] % CAP
        out[d, pl.ds(pl.multiple_of(k * TILE, TILE), TILE), :] = tiles[m]
        return carry

    out[:, CAP * TILE :, :] = meta[...]
    lax.fori_loop(0, live[0], put, 0)


def pack(place, live, tiles, meta):
    devices = meta.shape[0]
    vmem = pl.BlockSpec(memory_space=pltpu.VMEM)
    smem = pl.BlockSpec(memory_space=pltpu.SMEM)
    return pl.pallas_call(
        pack_kernel,
        out_shape=jax.ShapeDtypeStruct((devices, CAP * TILE + META, TILE), f32),
        in_specs=[smem, smem, vmem, vmem],
        out_specs=vmem,
        compiler_params=pltpu.CompilerParams(vmem_limit_bytes=16 * MIB),
        name="pack",
    )(place, live, tiles, meta)


def add_kernel(panel, *refs):
    if panel:
        arrived, out, landing, buf, where_to, sem, head, places, head_sem = refs
        slots = arrived.shape[0] * CAP
        copy = pltpu.make_async_copy(arrived.at[:, CAP * TILE :, :], head, head_sem)
        copy.start()
        copy.wait()
        places[...] = jnp.sum(head[...], axis=0).astype(i32) - 1
        copy = pltpu.make_async_copy(places, landing, head_sem)
        copy.start()
        out[...] = jnp.zeros_like(out)
        copy.wait()
    else:
        landing, arrived, out, buf, where_to, sem = refs
        slots = arrived.shape[0] * CAP

    def fetch(k, n):
        pair, turn = k // CAP, k % CAP
        rows = pl.ds(pl.multiple_of(turn * TILE, TILE), TILE)
        return pltpu.make_async_copy(arrived.at[pair, rows, :], buf.at[n], sem)

    def scan(k, n):
        t = landing[k % CAP, k // CAP]
        hit = (t >= 0) & (t % LCOLS == 0) if panel else t >= 0

        @pl.when(hit)
        def _():
            where_to[n] = t
            fetch(k, n).start()

        return n + hit.astype(i32)

    count = lax.fori_loop(0, slots, scan, 0, unroll=8)
    if not panel:
        out[...] = jnp.zeros_like(out)
    lax.fori_loop(0, count, lambda n, c: (fetch(0, n).wait(), c)[1], 0)

    def add(n, c):
        t = where_to[n]
        if panel:
            a = t // LCOLS
            out[a] = out[a] + buf[n]
        else:
            a, b = t // LCOLS, t % LCOLS
            out[a, b] = out[a, b] + buf[n]
        return c

    lax.fori_loop(0, count, add, 0)


def add_up(panel, arrived, landing=None):
    devices = arrived.shape[0]
    vmem = pl.BlockSpec(memory_space=pltpu.VMEM)
    smem = pl.BlockSpec(memory_space=pltpu.SMEM)
    scratch = [
        pltpu.VMEM((devices * CAP, TILE, TILE), f32),
        pltpu.SMEM((devices * CAP,), i32),
        pltpu.SemaphoreType.DMA,
    ]
    any_space = pl.BlockSpec(memory_space=pl.ANY)
    if panel:
        return pl.pallas_call(
            functools.partial(add_kernel, True),
            out_shape=[
                jax.ShapeDtypeStruct((LROWS, TILE, TILE), f32),
                jax.ShapeDtypeStruct((META, devices), i32),
            ],
            in_specs=[any_space],
            out_specs=[vmem, smem],
            scratch_shapes=scratch
            + [
                pltpu.VMEM((devices, META, TILE), f32),
                pltpu.VMEM((META, devices), i32),
                pltpu.SemaphoreType.DMA,
            ],
            compiler_params=pltpu.CompilerParams(vmem_limit_bytes=56 * MIB),
            name="add_panel",
        )(arrived)
    return pl.pallas_call(
        functools.partial(add_kernel, False),
        out_shape=jax.ShapeDtypeStruct((LROWS, LCOLS, TILE, TILE), f32),
        in_specs=[smem, any_space],
        out_specs=vmem,
        scratch_shapes=scratch,
        compiler_params=pltpu.CompilerParams(vmem_limit_bytes=30 * MIB),
        cost_estimate=pl.CostEstimate(
            flops=1000, bytes_accessed=24 * MIB, transcendentals=0
        ),
        name="add_all",
    )(landing, arrived)


BLOCK = 256
KB = 3 * BLOCK
KP = 3 * PANEL


def left_form(ref, lane, x):
    hi, lo = split(x)
    for k in range(x.shape[1] // BLOCK):
        for part, half in enumerate((hi, hi, lo)):
            at = lane + (3 * k + part) * BLOCK
            ref[:, at : at + BLOCK] = half[:, k * BLOCK : (k + 1) * BLOCK]


def right_rows(ref, x):
    hi, lo = split(x)
    for k in range(x.shape[1] // BLOCK):
        for part, half in enumerate((hi, lo, hi)):
            at = (3 * k + part) * BLOCK
            ref[:, at : at + BLOCK] = half[:, k * BLOCK : (k + 1) * BLOCK]


def right_columns(ref, x):
    hi, lo = split(x)
    for k in range(x.shape[0] // BLOCK):
        for part, half in enumerate((hi, lo, hi)):
            at = (3 * k + part) * BLOCK
            ref[at : at + BLOCK, :] = half[k * BLOCK : (k + 1) * BLOCK, :]


def times(a, b):
    return jnp.dot(a, b, preferred_element_type=f32)


def times_transposed(a, b):
    return lax.dot_general(a, b, (((1,), (1,)), ((), ())), preferred_element_type=f32)


def inverse_transposed(x, w):
    return times_transposed(x[:, :KB], w[:BLOCK, :KB]), times_transposed(x[...], w[BLOCK:, :])


def inverse(x, w):
    return times(x[...], w[:, :BLOCK]), times(x[:, KB:], w[KB:, BLOCK:])


def row_factors(at, pieces, corner, inverses, z, own, f0, f1, left, r_rows, r_cols, low):
    dz, xh = at[3], at[4]
    row = (at[0] * 4 + at[1]) * 2 + at[2]
    col = dz * 2 + xh
    around = lambda d, other: (dz + d + 4) % 4 * 2 + (1 - xh if other else xh)
    here, up, down, far, far2 = pieces
    for piece, first, source in (
        (here, 0, around(0, False)),
        (here, 8, around(0, True)),
        (up, 0, around(-1, False)),
        (up, 8, around(-1, True)),
        (down, 0, around(1, False)),
        (down, 8, around(1, True)),
        (far, 0, around(2, False)),
        (far2, 0, around(2, True)),
    ):
        lanes = pl.ds(pl.multiple_of(source % PT * TILE, TILE), TILE)
        for panel, ref in enumerate((f0, f1)):

            @pl.when(source // PT == panel)
            def _():
                for a in range(LROWS):
                    ref[a * TILE : (a + 1) * TILE, lanes] = piece[first + a]

    tile = jnp.where(lax.broadcasted_iota(i32, (LROWS * TILE, 1), 0) < TILE, row, NF)
    my_lanes = pl.ds(pl.multiple_of(col % PT * TILE, TILE), TILE)

    def keep(ref, tiles):
        for a in range(tiles):
            own[a] = ref[a * TILE : (a + 1) * TILE, my_lanes]

    right_rows(r_rows, inverses[0])
    y_bit = jnp.where(at[1] >= 2, at[1], 3 - at[1]) - 2
    for k in range(PT):
        i = (y_bit ^ (k & 1)) * 2 + (at[2] ^ (k >> 1))
        rows = pl.ds(pl.multiple_of(i * TILE, TILE), TILE)
        for j in range(PT):
            here = corner[k >> 1][(k & 1) * PT + j]
            low[rows, j * TILE : (j + 1) * TILE] = here
    left_form(left.at[:PANEL], 0, low[...])
    one, two = inverse_transposed(left.at[:PANEL], r_rows)
    low[:, :BLOCK] = one
    low[:, BLOCK:] = two
    left_form(left, 0, f0[...])
    one, two = inverse_transposed(left, r_rows)
    f0[:, :BLOCK] = jnp.where(tile >= PT, one, 0.0)
    f0[:, BLOCK:] = jnp.where(tile >= PT, two, 0.0)

    @pl.when(col < PT)
    def _():
        keep(f0, LROWS)

    left_form(left, 0, f0[...])
    right_rows(r_rows, low[...])
    f1[...] = f1[...] - times_transposed(left[...], r_rows[...])

    @pl.when(col >= PT)
    def _():
        keep(f1, 1)

    left_form(left, 0, f1[...])
    right_rows(r_rows, inverses[1])
    one, two = inverse_transposed(left, r_rows)
    f1[:, :BLOCK] = jnp.where(tile >= 2 * PT, one, 0.0)
    f1[:, BLOCK:] = jnp.where(tile >= 2 * PT, two, 0.0)

    @pl.when(col >= PT)
    def _():
        for a in range(1, LROWS):
            own[a] = f1[a * TILE : (a + 1) * TILE, my_lanes]

        @pl.when(row >= 2 * PT)
        def _():
            own[0] = f1[:TILE, my_lanes]

    left_form(left, 0, f1[...])
    right_columns(r_cols, inverses[1])
    one, two = inverse(left, r_cols)
    f1[:, :BLOCK] = one
    f1[:, BLOCK:] = two
    left_form(z, KP, f1[...])
    right_columns(r_cols, low[...])
    f0[...] = f0[...] - times(z[:, KP:], r_cols[...])
    left_form(left, 0, f0[...])
    right_columns(r_cols, inverses[0])
    one, two = inverse(left, r_cols)
    f0[:, :BLOCK] = one
    f0[:, BLOCK:] = two
    left_form(z, 0, f0[...])


def update_kernel(
    at, *refs
):
    columns, pieces, corner = refs[:10], refs[10:15], refs[15:17]
    front, inverses, out = refs[17:20]
    z, right, raw, own, f0, f1, r_rows, r_cols, low = refs[20:]
    left = z.at[:, :KP]
    step = pl.program_id(0)

    @pl.when(step == 0)
    def _():
        row_factors(
            at, pieces, corner, inverses, z, own, f0, f1, left, r_rows, r_cols, low
        )

    for k in range(2):
        core = at[2] ^ k
        here, up, down, far, far2 = columns[5 * k : 5 * k + 5]
        for ref, n, other, dy in (
            (here, 0, 0, 0),
            (here, 1, 1, 0),
            (up, 0, 0, -1),
            (up, 1, 1, -1),
            (down, 0, 0, 1),
            (down, 1, 1, 1),
            (far, 0, 0, 2),
            (far2, 0, 1, 2),
        ):
            source = (at[1] + dy - at[3] + 8) % 4 * 2 + core
            rows = pl.ds(pl.multiple_of((at[0] ^ other) * TILE, TILE), TILE)
            lanes = pl.ds(pl.multiple_of(source * TILE, TILE), TILE)
            raw[rows, lanes] = ref[n * LROWS + step]
    right_rows(right, raw[...])
    change = times_transposed(z[...], right[...])
    for t in range(LROWS):
        for b in range(2):
            piece = change[t * TILE : (t + 1) * TILE, b * TILE : (b + 1) * TILE]
            out[t, b] = front[t, b] - piece

    @pl.when(step == 0)
    def _():
        for t in range(1, LROWS):
            out[t, 0] = own[t]

        @pl.when((at[0] * 4 + at[1]) * 2 + at[2] >= PT)
        def _():
            out[0, 0] = own[0]


def update(at, columns, front, pieces, corner, inverses):
    height = LROWS * TILE
    vmem = pl.BlockSpec(memory_space=pltpu.VMEM)
    block = pl.BlockSpec((LROWS, 2, TILE, TILE), lambda j: (0, j, 0, 0))
    return pl.pallas_call(
        update_kernel,
        grid=(LCOLS // 2,),
        out_shape=jax.ShapeDtypeStruct((LROWS, LCOLS, TILE, TILE), f32),
        in_specs=[
            pl.BlockSpec(memory_space=pltpu.SMEM),
            *[vmem] * 17,
            block,
            vmem,
        ],
        out_specs=block,
        scratch_shapes=[
            pltpu.VMEM((height, 2 * KP), bf16),
            pltpu.VMEM((2 * TILE, 2 * KP), bf16),
            pltpu.VMEM((2 * TILE, WIDE), f32),
            pltpu.VMEM((LROWS, TILE, TILE), f32),
            pltpu.VMEM((height, PANEL), f32),
            pltpu.VMEM((height, PANEL), f32),
            pltpu.VMEM((PANEL, KP), bf16),
            pltpu.VMEM((KP, PANEL), bf16),
            pltpu.VMEM((PANEL, PANEL), f32),
        ],
        compiler_params=pltpu.CompilerParams(vmem_limit_bytes=32 * MIB),
        cost_estimate=pl.CostEstimate(
            flops=24_000_000_000, bytes_accessed=30 * MIB, transcendentals=0
        ),
        name="update",
    )(at, *columns, *pieces, *corner, front, inverses)


def move(x, axis, size, to):
    return lax.ppermute(x, axis, [(i, to(i)) for i in range(size)])


def both_ways(own, axis):
    up, down = lambda i: (i + 2) % 8, lambda i: (i - 2) % 8
    return [move(own, axis, 8, up), move(own, axis, 8, down)]


def opposite(before, behind, axis):
    half = before.shape[0] // 2
    up, down = lambda i: (i + 2) % 8, lambda i: (i - 2) % 8
    return [move(before[:half], axis, 8, up), move(behind[half:], axis, 8, down)]


def gather_corner(top):
    sib, row = lax.axis_index("sib"), lax.axis_index("row")
    flip = [(4, 2), (5, 3), (6, 0), (7, 1)]
    a = lax.ppermute(top, "sib", [(0, 1)])
    b = lax.ppermute(top, "row", flip)
    c = lax.ppermute(top, ("sib", "row"), [(i, 8 + j) for i, j in flip])
    mine = jnp.where(row >= 4, jnp.where(sib == 0, top, a), jnp.where(sib == 0, b, c))
    both = jnp.concatenate([mine, move(mine, "row", 8, lambda i: i ^ 2)], axis=0)
    return [both, move(both, "row", 8, lambda i: i ^ 1)]


def gather(panel, arrived, landing):
    there = []
    for y in range(4):
        for core in range(2):
            for z in range(4):
                for xh in range(2):
                    to = ((y + z) % 4 * 2 + xh) * 8 + y * 2 + core
                    there.append(((y * 2 + core) * 8 + z * 2 + xh, to))
    across = lax.ppermute(panel, ("row", "col"), there)
    pair = jnp.concatenate([panel, move(panel, "col", 8, lambda i: i ^ 1)], axis=0)
    top = jnp.broadcast_to(panel[:1], (8, TILE, TILE))
    top = lax.all_to_all(top, "col", split_axis=0, concat_axis=0, tiled=True)[:PT]
    pair, top, across = lax.optimization_barrier((pair, top, across))
    other = move(across, "sib", 2, lambda i: 1 - i)
    pieces = [pair, *both_ways(pair, "col")]
    across, other, top = lax.optimization_barrier((across, other, top))
    columns = [jnp.concatenate([across, other], axis=0)]
    columns += both_ways(columns[0], "row")
    corner = gather_corner(top)
    *columns, front = lax.optimization_barrier((*columns, add_up(False, arrived, landing)))
    columns += opposite(*columns[1:], "row")
    pieces += opposite(*pieces[1:], "col")
    columns += [move(x, "row", 8, lambda i: i ^ 1) for x in columns]
    return columns, pieces, corner, front


def local(child_tiles, child_rows, child_slots, tile_count, inverses):
    grid_rows = lax.axis_size("sib") * lax.axis_size("row")
    columns = lax.axis_size("col")
    devices = grid_rows * columns
    slot_ids = child_slots[0, 0]
    live = tile_count[0]
    row_list = child_rows[0]
    child_row, child_col = slot_ids // CHILD_TILES, slot_ids % CHILD_TILES
    positions = jnp.arange(CHILD_TILES, dtype=i32)
    lookup = lambda x: jnp.sum(
        jnp.where(x[:, None] == positions[None, :], row_list[None, :], 0), axis=1
    )
    parent_row, parent_col = lookup(child_row), lookup(child_col)
    owner = parent_row % grid_rows * columns + parent_col % columns
    target = parent_row // grid_rows * LCOLS + parent_col // columns
    order = jnp.arange(slot_ids.shape[0], dtype=i32)
    is_live = order < live
    earlier = (
        (owner[:, None] == owner[None, :])
        & is_live[None, :]
        & (order[None, :] < order[:, None])
    )
    rank = jnp.sum(earlier.astype(i32), axis=1)
    place = jnp.where(is_live, owner * CAP + rank, devices * CAP)
    filled = place[None, :] == jnp.arange(devices * CAP, dtype=i32)[:, None]
    destined = jnp.sum(jnp.where(filled, target[None, :] + 1, 0), axis=1)
    me = lax.axis_index(("sib", "row", "col"))
    mine = jnp.arange(devices, dtype=i32) == me
    meta = jnp.where(mine, destined.reshape(devices, CAP, 1), 0).astype(f32)
    meta = jnp.pad(meta, ((0, 0), (0, META - CAP), (0, 0)))
    outgoing = pack(place, live, child_tiles[0, 0], meta)
    arrived = lax.all_to_all(
        outgoing, ("sib", "row", "col"), split_axis=0, concat_axis=0, tiled=True
    )
    panel, landing = add_up(True, arrived)
    columns, pieces, corner, front = gather(panel, arrived, landing)
    row = lax.axis_index("row")
    col = lax.axis_index("col")
    at = jnp.stack([lax.axis_index("sib"), row // 2, row % 2, col // 2, col % 2])
    at = at.astype(i32)
    out = update(at, columns, front, pieces, corner, inverses)
    return out.reshape(LROWS, 1, LCOLS, 1, TILE, TILE)


def solution(mesh):
    return jax.shard_map(
        local,
        mesh=mesh,
        in_specs=(
            P("sib", ("row", "col"), None, None, None),
            P("sib", None),
            P("sib", ("row", "col"), None),
            P("sib", ("row", "col")),
            P(),
        ),
        out_specs=P(None, ("sib", "row"), None, "col", None, None),
        check_vma=False,
    )
```

```python
import functools

import jax
import jax.numpy as jnp
from jax import lax
from jax.experimental import pallas as pl
from jax.experimental.pallas import tpu as pltpu
from jax.sharding import PartitionSpec as P

NF = 16384
TILE = 128
PANEL = 512
NPANEL = 2
CHILD_TILES = 64
CAP = 2
PT = PANEL // TILE
WIDE = NPANEL * PANEL
META = 8
LROWS, LCOLS = 8, 16
f32, bf16, i32 = jnp.float32, jnp.bfloat16, jnp.int32
MIB = 1 << 20


def split(x):
    hi = x.astype(bf16)
    return hi, (x - hi.astype(f32)).astype(bf16)


def pack_kernel(place, live, tiles, meta, out):
    def put(m, carry):
        d = place[m] // CAP
        k = place[m] % CAP
        out[d, pl.ds(pl.multiple_of(k * TILE, TILE), TILE), :] = tiles[m]
        return carry

    out[:, CAP * TILE :, :] = meta[...]
    lax.fori_loop(0, live[0], put, 0)


def pack(place, live, tiles, meta):
    devices = meta.shape[0]
    vmem = pl.BlockSpec(memory_space=pltpu.VMEM)
    smem = pl.BlockSpec(memory_space=pltpu.SMEM)
    return pl.pallas_call(
        pack_kernel,
        out_shape=jax.ShapeDtypeStruct((devices, CAP * TILE + META, TILE), f32),
        in_specs=[smem, smem, vmem, vmem],
        out_specs=vmem,
        compiler_params=pltpu.CompilerParams(vmem_limit_bytes=16 * MIB),
        name="pack",
    )(place, live, tiles, meta)


def add_kernel(panel, *refs):
    if panel:
        arrived, out, landing, buf, where_to, sem, head, places, head_sem = refs
        slots = arrived.shape[0] * CAP
        copy = pltpu.make_async_copy(arrived.at[:, CAP * TILE :, :], head, head_sem)
        copy.start()
        copy.wait()
        places[...] = jnp.sum(head[...], axis=0).astype(i32) - 1
        copy = pltpu.make_async_copy(places, landing, head_sem)
        copy.start()
        out[...] = jnp.zeros_like(out)
        copy.wait()
    else:
        landing, arrived, out, buf, where_to, sem = refs
        slots = arrived.shape[0] * CAP

    def fetch(k, n):
        pair, turn = k // CAP, k % CAP
        rows = pl.ds(pl.multiple_of(turn * TILE, TILE), TILE)
        return pltpu.make_async_copy(arrived.at[pair, rows, :], buf.at[n], sem)

    def scan(k, n):
        t = landing[k % CAP, k // CAP]
        hit = (t >= 0) & (t % LCOLS == 0) if panel else t >= 0

        @pl.when(hit)
        def _():
            where_to[n] = t
            fetch(k, n).start()

        return n + hit.astype(i32)

    count = lax.fori_loop(0, slots, scan, 0, unroll=8)
    if not panel:
        out[...] = jnp.zeros_like(out)
    lax.fori_loop(0, count, lambda n, c: (fetch(0, n).wait(), c)[1], 0)

    def add(n, c):
        t = where_to[n]
        if panel:
            a = t // LCOLS
            out[a] = out[a] + buf[n]
        else:
            a, b = t // LCOLS, t % LCOLS
            out[a, b] = out[a, b] + buf[n]
        return c

    lax.fori_loop(0, count, add, 0)


def add_up(panel, arrived, landing=None):
    devices = arrived.shape[0]
    vmem = pl.BlockSpec(memory_space=pltpu.VMEM)
    smem = pl.BlockSpec(memory_space=pltpu.SMEM)
    scratch = [
        pltpu.VMEM((devices * CAP, TILE, TILE), f32),
        pltpu.SMEM((devices * CAP,), i32),
        pltpu.SemaphoreType.DMA,
    ]
    any_space = pl.BlockSpec(memory_space=pl.ANY)
    if panel:
        return pl.pallas_call(
            functools.partial(add_kernel, True),
            out_shape=[
                jax.ShapeDtypeStruct((LROWS, TILE, TILE), f32),
                jax.ShapeDtypeStruct((META, devices), i32),
            ],
            in_specs=[any_space],
            out_specs=[vmem, smem],
            scratch_shapes=scratch
            + [
                pltpu.VMEM((devices, META, TILE), f32),
                pltpu.VMEM((META, devices), i32),
                pltpu.SemaphoreType.DMA,
            ],
            compiler_params=pltpu.CompilerParams(vmem_limit_bytes=56 * MIB),
            name="add_panel",
        )(arrived)
    return pl.pallas_call(
        functools.partial(add_kernel, False),
        out_shape=jax.ShapeDtypeStruct((LROWS, LCOLS, TILE, TILE), f32),
        in_specs=[smem, any_space],
        out_specs=vmem,
        scratch_shapes=scratch,
        compiler_params=pltpu.CompilerParams(vmem_limit_bytes=30 * MIB),
        cost_estimate=pl.CostEstimate(
            flops=1000, bytes_accessed=24 * MIB, transcendentals=0
        ),
        name="add_all",
    )(landing, arrived)


BLOCK = 256
KB = 3 * BLOCK
KP = 3 * PANEL


def left_form(ref, lane, x):
    hi, lo = split(x)
    for k in range(x.shape[1] // BLOCK):
        for part, half in enumerate((hi, hi, lo)):
            at = lane + (3 * k + part) * BLOCK
            ref[:, at : at + BLOCK] = half[:, k * BLOCK : (k + 1) * BLOCK]


def right_rows(ref, x):
    hi, lo = split(x)
    for k in range(x.shape[1] // BLOCK):
        for part, half in enumerate((hi, lo, hi)):
            at = (3 * k + part) * BLOCK
            ref[:, at : at + BLOCK] = half[:, k * BLOCK : (k + 1) * BLOCK]


def right_columns(ref, x):
    hi, lo = split(x)
    for k in range(x.shape[0] // BLOCK):
        for part, half in enumerate((hi, lo, hi)):
            at = (3 * k + part) * BLOCK
            ref[at : at + BLOCK, :] = half[k * BLOCK : (k + 1) * BLOCK, :]


def times(a, b):
    return jnp.dot(a, b, preferred_element_type=f32)


def times_transposed(a, b):
    return lax.dot_general(a, b, (((1,), (1,)), ((), ())), preferred_element_type=f32)


def inverse_transposed(x, w):
    return times_transposed(x[:, :KB], w[:BLOCK, :KB]), times_transposed(x[...], w[BLOCK:, :])


def inverse(x, w):
    return times(x[...], w[:, :BLOCK]), times(x[:, KB:], w[KB:, BLOCK:])


def row_factors(at, pieces, corner, inverses, z, own, f0, f1, left, r_rows, r_cols, low):
    dz, xh = at[3], at[4]
    row = (at[0] * 4 + at[1]) * 2 + at[2]
    col = dz * 2 + xh
    around = lambda d, other: (dz + d + 4) % 4 * 2 + (1 - xh if other else xh)
    here, up, down, far, far2 = pieces
    for piece, first, source in (
        (here, 0, around(0, False)),
        (here, 8, around(0, True)),
        (up, 0, around(-1, False)),
        (up, 8, around(-1, True)),
        (down, 0, around(1, False)),
        (down, 8, around(1, True)),
        (far, 0, around(2, False)),
        (far2, 0, around(2, True)),
    ):
        lanes = pl.ds(pl.multiple_of(source % PT * TILE, TILE), TILE)
        for panel, ref in enumerate((f0, f1)):

            @pl.when(source // PT == panel)
            def _():
                for a in range(LROWS):
                    ref[a * TILE : (a + 1) * TILE, lanes] = piece[first + a]

    tile = jnp.where(lax.broadcasted_iota(i32, (LROWS * TILE, 1), 0) < TILE, row, NF)
    my_lanes = pl.ds(pl.multiple_of(col % PT * TILE, TILE), TILE)

    def keep(ref, tiles):
        for a in range(tiles):
            own[a] = ref[a * TILE : (a + 1) * TILE, my_lanes]

    right_rows(r_rows, inverses[0])
    y_bit = jnp.where(at[1] >= 2, at[1], 3 - at[1]) - 2
    for k in range(PT):
        i = (y_bit ^ (k & 1)) * 2 + (at[2] ^ (k >> 1))
        rows = pl.ds(pl.multiple_of(i * TILE, TILE), TILE)
        for j in range(PT):
            here = corner[k >> 1][(k & 1) * PT + j]
            low[rows, j * TILE : (j + 1) * TILE] = here
    left_form(left.at[:PANEL], 0, low[...])
    one, two = inverse_transposed(left.at[:PANEL], r_rows)
    low[:, :BLOCK] = one
    low[:, BLOCK:] = two
    left_form(left, 0, f0[...])
    one, two = inverse_transposed(left, r_rows)
    f0[:, :BLOCK] = jnp.where(tile >= PT, one, 0.0)
    f0[:, BLOCK:] = jnp.where(tile >= PT, two, 0.0)

    @pl.when(col < PT)
    def _():
        keep(f0, LROWS)

    left_form(left, 0, f0[...])
    right_rows(r_rows, low[...])
    f1[...] = f1[...] - times_transposed(left[...], r_rows[...])

    @pl.when(col >= PT)
    def _():
        keep(f1, 1)

    left_form(left, 0, f1[...])
    right_rows(r_rows, inverses[1])
    one, two = inverse_transposed(left, r_rows)
    f1[:, :BLOCK] = jnp.where(tile >= 2 * PT, one, 0.0)
    f1[:, BLOCK:] = jnp.where(tile >= 2 * PT, two, 0.0)

    @pl.when(col >= PT)
    def _():
        for a in range(1, LROWS):
            own[a] = f1[a * TILE : (a + 1) * TILE, my_lanes]

        @pl.when(row >= 2 * PT)
        def _():
            own[0] = f1[:TILE, my_lanes]

    left_form(left, 0, f1[...])
    right_columns(r_cols, inverses[1])
    one, two = inverse(left, r_cols)
    f1[:, :BLOCK] = one
    f1[:, BLOCK:] = two
    left_form(z, KP, f1[...])
    right_columns(r_cols, low[...])
    f0[...] = f0[...] - times(z[:, KP:], r_cols[...])
    left_form(left, 0, f0[...])
    right_columns(r_cols, inverses[0])
    one, two = inverse(left, r_cols)
    f0[:, :BLOCK] = one
    f0[:, BLOCK:] = two
    left_form(z, 0, f0[...])


def update_kernel(
    at, *refs
):
    columns, pieces, corner = refs[:10], refs[10:15], refs[15:17]
    front, inverses, out = refs[17:20]
    z, right, raw, own, f0, f1, r_rows, r_cols, low = refs[20:]
    left = z.at[:, :KP]
    step = pl.program_id(0)

    @pl.when(step == 0)
    def _():
        row_factors(
            at, pieces, corner, inverses, z, own, f0, f1, left, r_rows, r_cols, low
        )

    for k in range(2):
        core = at[2] ^ k
        here, up, down, far, far2 = columns[5 * k : 5 * k + 5]
        for ref, n, other, dy in (
            (here, 0, 0, 0),
            (here, 1, 1, 0),
            (up, 0, 0, -1),
            (up, 1, 1, -1),
            (down, 0, 0, 1),
            (down, 1, 1, 1),
            (far, 0, 0, 2),
            (far2, 0, 1, 2),
        ):
            source = (at[1] + dy - at[3] + 8) % 4 * 2 + core
            rows = pl.ds(pl.multiple_of((at[0] ^ other) * TILE, TILE), TILE)
            lanes = pl.ds(pl.multiple_of(source * TILE, TILE), TILE)
            raw[rows, lanes] = ref[n, 0]
    right_rows(right, raw[...])
    change = times_transposed(z[...], right[...])
    for t in range(LROWS):
        for b in range(2):
            piece = change[t * TILE : (t + 1) * TILE, b * TILE : (b + 1) * TILE]
            out[t, b] = front[t, b] - piece

    @pl.when(step == 0)
    def _():
        for t in range(1, LROWS):
            out[t, 0] = own[t]

        @pl.when((at[0] * 4 + at[1]) * 2 + at[2] >= PT)
        def _():
            out[0, 0] = own[0]


def update(at, columns, front, pieces, corner, inverses):
    height = LROWS * TILE
    vmem = pl.BlockSpec(memory_space=pltpu.VMEM)
    block = pl.BlockSpec((LROWS, 2, TILE, TILE), lambda j: (0, j, 0, 0))
    return pl.pallas_call(
        update_kernel,
        grid=(LCOLS // 2,),
        out_shape=jax.ShapeDtypeStruct((LROWS, LCOLS, TILE, TILE), f32),
        in_specs=[
            pl.BlockSpec(memory_space=pltpu.SMEM),
            *(
                pl.BlockSpec((x.shape[0], 1, TILE, TILE), lambda j: (0, j, 0, 0))
                for x in columns
            ),
            *[vmem] * 7,
            block,
            vmem,
        ],
        out_specs=block,
        scratch_shapes=[
            pltpu.VMEM((height, 2 * KP), bf16),
            pltpu.VMEM((2 * TILE, 2 * KP), bf16),
            pltpu.VMEM((2 * TILE, WIDE), f32),
            pltpu.VMEM((LROWS, TILE, TILE), f32),
            pltpu.VMEM((height, PANEL), f32),
            pltpu.VMEM((height, PANEL), f32),
            pltpu.VMEM((PANEL, KP), bf16),
            pltpu.VMEM((KP, PANEL), bf16),
            pltpu.VMEM((PANEL, PANEL), f32),
        ],
        compiler_params=pltpu.CompilerParams(vmem_limit_bytes=36 * MIB),
        cost_estimate=pl.CostEstimate(
            flops=24_000_000_000, bytes_accessed=30 * MIB, transcendentals=0
        ),
        name="update",
    )(at, *columns, *pieces, *corner, front, inverses)


def move(x, axis, size, to):
    return lax.ppermute(x, axis, [(i, to(i)) for i in range(size)])


def both_ways(own, axis):
    up, down = lambda i: (i + 2) % 8, lambda i: (i - 2) % 8
    return [move(own, axis, 8, up), move(own, axis, 8, down)]


def opposite(before, behind, axis):
    half = before.shape[0] // 2
    up, down = lambda i: (i + 2) % 8, lambda i: (i - 2) % 8
    return [move(before[:half], axis, 8, up), move(behind[half:], axis, 8, down)]


def gather_corner(top):
    sib, row = lax.axis_index("sib"), lax.axis_index("row")
    flip = [(4, 2), (5, 3), (6, 0), (7, 1)]
    a = lax.ppermute(top, "sib", [(0, 1)])
    b = lax.ppermute(top, "row", flip)
    c = lax.ppermute(top, ("sib", "row"), [(i, 8 + j) for i, j in flip])
    mine = jnp.where(row >= 4, jnp.where(sib == 0, top, a), jnp.where(sib == 0, b, c))
    return jnp.concatenate([mine, move(mine, "row", 8, lambda i: i ^ 2)], axis=0)


def gather(panel, arrived, landing):
    there = []
    for y in range(4):
        for core in range(2):
            for z in range(4):
                for xh in range(2):
                    to = ((y + z) % 4 * 2 + xh) * 8 + y * 2 + core
                    there.append(((y * 2 + core) * 8 + z * 2 + xh, to))
    across = lax.ppermute(panel, ("row", "col"), there)
    pair = jnp.concatenate([panel, move(panel, "col", 8, lambda i: i ^ 1)], axis=0)
    top = jnp.broadcast_to(panel[:1], (8, TILE, TILE))
    top = lax.all_to_all(top, "col", split_axis=0, concat_axis=0, tiled=True)[:PT]
    pair, top, across = lax.optimization_barrier((pair, top, across))
    pieces = [pair, *both_ways(pair, "col")]
    pieces += opposite(*pieces[1:], "col")
    corner = gather_corner(top)
    pair = jnp.concatenate([across, move(across, "sib", 2, lambda i: 1 - i)], axis=0)
    pair, corner = lax.optimization_barrier((pair, corner))
    columns = [pair, *both_ways(pair, "row")]
    corner = [corner, move(corner, "row", 8, lambda i: i ^ 1)]
    front = add_up(False, arrived, landing)
    *columns, front = lax.optimization_barrier((*columns, front))
    columns += opposite(*columns[1:], "row")
    columns = columns + [move(x, "row", 8, lambda i: i ^ 1) for x in columns]
    columns = [x.reshape(-1, LROWS, TILE, TILE) for x in columns]
    return columns, pieces, corner, front


def local(child_tiles, child_rows, child_slots, tile_count, inverses):
    grid_rows = lax.axis_size("sib") * lax.axis_size("row")
    columns = lax.axis_size("col")
    devices = grid_rows * columns
    slot_ids = child_slots[0, 0]
    live = tile_count[0]
    row_list = child_rows[0]
    child_row, child_col = slot_ids // CHILD_TILES, slot_ids % CHILD_TILES
    positions = jnp.arange(CHILD_TILES, dtype=i32)
    lookup = lambda x: jnp.sum(
        jnp.where(x[:, None] == positions[None, :], row_list[None, :], 0), axis=1
    )
    parent_row, parent_col = lookup(child_row), lookup(child_col)
    owner = parent_row % grid_rows * columns + parent_col % columns
    target = parent_row // grid_rows * LCOLS + parent_col // columns
    order = jnp.arange(slot_ids.shape[0], dtype=i32)
    is_live = order < live
    earlier = (
        (owner[:, None] == owner[None, :])
        & is_live[None, :]
        & (order[None, :] < order[:, None])
    )
    rank = jnp.sum(earlier.astype(i32), axis=1)
    place = jnp.where(is_live, owner * CAP + rank, devices * CAP)
    filled = place[None, :] == jnp.arange(devices * CAP, dtype=i32)[:, None]
    destined = jnp.sum(jnp.where(filled, target[None, :] + 1, 0), axis=1)
    me = lax.axis_index(("sib", "row", "col"))
    mine = jnp.arange(devices, dtype=i32) == me
    meta = jnp.where(mine, destined.reshape(devices, CAP, 1), 0).astype(f32)
    meta = jnp.pad(meta, ((0, 0), (0, META - CAP), (0, 0)))
    outgoing = pack(place, live, child_tiles[0, 0], meta)
    arrived = lax.all_to_all(
        outgoing, ("sib", "row", "col"), split_axis=0, concat_axis=0, tiled=True
    )
    panel, landing = add_up(True, arrived)
    columns, pieces, corner, front = gather(panel, arrived, landing)
    row = lax.axis_index("row")
    col = lax.axis_index("col")
    at = jnp.stack([lax.axis_index("sib"), row // 2, row % 2, col // 2, col % 2])
    at = at.astype(i32)
    out = update(at, columns, front, pieces, corner, inverses)
    return out.reshape(LROWS, 1, LCOLS, 1, TILE, TILE)


def solution(mesh):
    return jax.shard_map(
        local,
        mesh=mesh,
        in_specs=(
            P("sib", ("row", "col"), None, None, None),
            P("sib", None),
            P("sib", ("row", "col"), None),
            P("sib", ("row", "col")),
            P(),
        ),
        out_specs=P(None, ("sib", "row"), None, "col", None, None),
        check_vma=False,
    )
```

```python
import functools

import jax
import jax.numpy as jnp
from jax import lax
from jax.experimental import pallas as pl
from jax.experimental.pallas import tpu as pltpu
from jax.sharding import PartitionSpec as P

NF = 16384
TILE = 128
PANEL = 512
NPANEL = 2
CHILD_TILES = 64
CAP = 2
PT = PANEL // TILE
WIDE = NPANEL * PANEL
META = 8
LROWS, LCOLS = 8, 16
f32, bf16, i32 = jnp.float32, jnp.bfloat16, jnp.int32
MIB = 1 << 20


def split(x):
    hi = x.astype(bf16)
    return hi, (x - hi.astype(f32)).astype(bf16)


def pack_kernel(place, live, tiles, meta, out):
    def put(m, carry):
        d = place[m] // CAP
        k = place[m] % CAP
        out[d, pl.ds(pl.multiple_of(k * TILE, TILE), TILE), :] = tiles[m]
        return carry

    out[:, CAP * TILE :, :] = meta[...]
    lax.fori_loop(0, live[0], put, 0)


def pack(place, live, tiles, meta):
    devices = meta.shape[0]
    vmem = pl.BlockSpec(memory_space=pltpu.VMEM)
    smem = pl.BlockSpec(memory_space=pltpu.SMEM)
    return pl.pallas_call(
        pack_kernel,
        out_shape=jax.ShapeDtypeStruct((devices, CAP * TILE + META, TILE), f32),
        in_specs=[smem, smem, vmem, vmem],
        out_specs=vmem,
        compiler_params=pltpu.CompilerParams(vmem_limit_bytes=16 * MIB),
        name="pack",
    )(place, live, tiles, meta)


def add_kernel(panel, *refs):
    if panel:
        arrived, out, landing, buf, where_to, sem, head, places, head_sem = refs
        slots = arrived.shape[0] * CAP
        copy = pltpu.make_async_copy(arrived.at[:, CAP * TILE :, :], head, head_sem)
        copy.start()
        copy.wait()
        places[...] = jnp.sum(head[...], axis=0).astype(i32) - 1
        copy = pltpu.make_async_copy(places, landing, head_sem)
        copy.start()
        out[...] = jnp.zeros_like(out)
        copy.wait()
    else:
        landing, arrived, out, buf, where_to, sem = refs
        slots = arrived.shape[0] * CAP

    def fetch(k, n):
        pair, turn = k // CAP, k % CAP
        rows = pl.ds(pl.multiple_of(turn * TILE, TILE), TILE)
        return pltpu.make_async_copy(arrived.at[pair, rows, :], buf.at[n], sem)

    def scan(k, n):
        t = landing[k % CAP, k // CAP]
        hit = (t >= 0) & (t % LCOLS == 0) if panel else t >= 0

        @pl.when(hit)
        def _():
            where_to[n] = t
            fetch(k, n).start()

        return n + hit.astype(i32)

    count = lax.fori_loop(0, slots, scan, 0, unroll=8)
    if not panel:
        out[...] = jnp.zeros_like(out)
    lax.fori_loop(0, count, lambda n, c: (fetch(0, n).wait(), c)[1], 0)

    def add(n, c):
        t = where_to[n]
        if panel:
            a = t // LCOLS
            out[a] = out[a] + buf[n]
        else:
            a, b = t // LCOLS, t % LCOLS
            out[a, b] = out[a, b] + buf[n]
        return c

    lax.fori_loop(0, count, add, 0)


def add_up(panel, arrived, landing=None):
    devices = arrived.shape[0]
    vmem = pl.BlockSpec(memory_space=pltpu.VMEM)
    smem = pl.BlockSpec(memory_space=pltpu.SMEM)
    scratch = [
        pltpu.VMEM((devices * CAP, TILE, TILE), f32),
        pltpu.SMEM((devices * CAP,), i32),
        pltpu.SemaphoreType.DMA,
    ]
    any_space = pl.BlockSpec(memory_space=pl.ANY)
    if panel:
        return pl.pallas_call(
            functools.partial(add_kernel, True),
            out_shape=[
                jax.ShapeDtypeStruct((LROWS, TILE, TILE), f32),
                jax.ShapeDtypeStruct((META, devices), i32),
            ],
            in_specs=[any_space],
            out_specs=[vmem, smem],
            scratch_shapes=scratch
            + [
                pltpu.VMEM((devices, META, TILE), f32),
                pltpu.VMEM((META, devices), i32),
                pltpu.SemaphoreType.DMA,
            ],
            compiler_params=pltpu.CompilerParams(vmem_limit_bytes=56 * MIB),
            name="add_panel",
        )(arrived)
    return pl.pallas_call(
        functools.partial(add_kernel, False),
        out_shape=jax.ShapeDtypeStruct((LROWS, LCOLS, TILE, TILE), f32),
        in_specs=[smem, any_space],
        out_specs=vmem,
        scratch_shapes=scratch,
        compiler_params=pltpu.CompilerParams(vmem_limit_bytes=30 * MIB),
        cost_estimate=pl.CostEstimate(
            flops=1000, bytes_accessed=24 * MIB, transcendentals=0
        ),
        name="add_all",
    )(landing, arrived)


BLOCK = 256
KB = 3 * BLOCK
KP = 3 * PANEL


def left_form(ref, lane, x):
    hi, lo = split(x)
    for k in range(x.shape[1] // BLOCK):
        for part, half in enumerate((hi, hi, lo)):
            at = lane + (3 * k + part) * BLOCK
            ref[:, at : at + BLOCK] = half[:, k * BLOCK : (k + 1) * BLOCK]


def right_rows(ref, x):
    hi, lo = split(x)
    for k in range(x.shape[1] // BLOCK):
        for part, half in enumerate((hi, lo, hi)):
            at = (3 * k + part) * BLOCK
            ref[:, at : at + BLOCK] = half[:, k * BLOCK : (k + 1) * BLOCK]


def right_columns(ref, x):
    hi, lo = split(x)
    for k in range(x.shape[0] // BLOCK):
        for part, half in enumerate((hi, lo, hi)):
            at = (3 * k + part) * BLOCK
            ref[at : at + BLOCK, :] = half[k * BLOCK : (k + 1) * BLOCK, :]


def times(a, b):
    return jnp.dot(a, b, preferred_element_type=f32)


def times_transposed(a, b):
    return lax.dot_general(a, b, (((1,), (1,)), ((), ())), preferred_element_type=f32)


def inverse_transposed(x, w):
    return times_transposed(x[:, :KB], w[:BLOCK, :KB]), times_transposed(x[...], w[BLOCK:, :])


def inverse(x, w):
    return times(x[...], w[:, :BLOCK]), times(x[:, KB:], w[KB:, BLOCK:])


def row_factors(at, pieces, corner, inverses, z, own, f0, f1, left, r_rows, r_cols, low):
    dz, xh = at[3], at[4]
    row = (at[0] * 4 + at[1]) * 2 + at[2]
    col = dz * 2 + xh
    around = lambda d, other: (dz + d + 4) % 4 * 2 + (1 - xh if other else xh)
    here, up, down, far, far2 = pieces
    for piece, first, source in (
        (here, 0, around(0, False)),
        (here, 8, around(0, True)),
        (up, 0, around(-1, False)),
        (up, 8, around(-1, True)),
        (down, 0, around(1, False)),
        (down, 8, around(1, True)),
        (far, 0, around(2, False)),
        (far2, 0, around(2, True)),
    ):
        lanes = pl.ds(pl.multiple_of(source % PT * TILE, TILE), TILE)
        for panel, ref in enumerate((f0, f1)):

            @pl.when(source // PT == panel)
            def _():
                for a in range(LROWS):
                    ref[a * TILE : (a + 1) * TILE, lanes] = piece[first + a]

    tile = jnp.where(lax.broadcasted_iota(i32, (LROWS * TILE, 1), 0) < TILE, row, NF)
    my_lanes = pl.ds(pl.multiple_of(col % PT * TILE, TILE), TILE)

    def keep(ref, tiles):
        for a in range(tiles):
            own[a] = ref[a * TILE : (a + 1) * TILE, my_lanes]

    right_rows(r_rows, inverses[0])
    y_bit = jnp.where(at[1] >= 2, at[1], 3 - at[1]) - 2
    for k in range(PT):
        i = (y_bit ^ (k & 1)) * 2 + (at[2] ^ (k >> 1))
        rows = pl.ds(pl.multiple_of(i * TILE, TILE), TILE)
        for j in range(PT):
            here = corner[k >> 1][(k & 1) * PT + j]
            low[rows, j * TILE : (j + 1) * TILE] = here
    left_form(left.at[:PANEL], 0, low[...])
    one, two = inverse_transposed(left.at[:PANEL], r_rows)
    low[:, :BLOCK] = one
    low[:, BLOCK:] = two
    left_form(left, 0, f0[...])
    one, two = inverse_transposed(left, r_rows)
    f0[:, :BLOCK] = jnp.where(tile >= PT, one, 0.0)
    f0[:, BLOCK:] = jnp.where(tile >= PT, two, 0.0)

    @pl.when(col < PT)
    def _():
        keep(f0, LROWS)

    left_form(left, 0, f0[...])
    right_rows(r_rows, low[...])
    f1[...] = f1[...] - times_transposed(left[...], r_rows[...])

    @pl.when(col >= PT)
    def _():
        keep(f1, 1)

    left_form(left, 0, f1[...])
    right_rows(r_rows, inverses[1])
    one, two = inverse_transposed(left, r_rows)
    f1[:, :BLOCK] = jnp.where(tile >= 2 * PT, one, 0.0)
    f1[:, BLOCK:] = jnp.where(tile >= 2 * PT, two, 0.0)

    @pl.when(col >= PT)
    def _():
        for a in range(1, LROWS):
            own[a] = f1[a * TILE : (a + 1) * TILE, my_lanes]

        @pl.when(row >= 2 * PT)
        def _():
            own[0] = f1[:TILE, my_lanes]

    left_form(left, 0, f1[...])
    right_columns(r_cols, inverses[1])
    one, two = inverse(left, r_cols)
    f1[:, :BLOCK] = one
    f1[:, BLOCK:] = two
    left_form(z, KP, f1[...])
    right_columns(r_cols, low[...])
    f0[...] = f0[...] - times(z[:, KP:], r_cols[...])
    left_form(left, 0, f0[...])
    right_columns(r_cols, inverses[0])
    one, two = inverse(left, r_cols)
    f0[:, :BLOCK] = one
    f0[:, BLOCK:] = two
    left_form(z, 0, f0[...])


def update_kernel(
    at, *refs
):
    columns, pieces, corner = refs[:10], refs[10:15], refs[15:17]
    front, inverses, out = refs[17:20]
    z, right, raw, own, f0, f1, r_rows, r_cols, low = refs[20:]
    left = z.at[:, :KP]
    step = pl.program_id(0)

    @pl.when(step == 0)
    def _():
        row_factors(
            at, pieces, corner, inverses, z, own, f0, f1, left, r_rows, r_cols, low
        )

    for k in range(2):
        core = at[2] ^ k
        here, up, down, far, far2 = columns[5 * k : 5 * k + 5]
        for ref, n, other, dy in (
            (here, 0, 0, 0),
            (here, 1, 1, 0),
            (up, 0, 0, -1),
            (up, 1, 1, -1),
            (down, 0, 0, 1),
            (down, 1, 1, 1),
            (far, 0, 0, 2),
            (far2, 0, 1, 2),
        ):
            source = (at[1] + dy - at[3] + 8) % 4 * 2 + core
            rows = pl.ds(pl.multiple_of((at[0] ^ other) * TILE, TILE), TILE)
            lanes = pl.ds(pl.multiple_of(source * TILE, TILE), TILE)
            raw[rows, lanes] = ref[n, 0]
    right_rows(right, raw[...])
    change = times_transposed(z[...], right[...])
    for t in range(LROWS):
        for b in range(2):
            piece = change[t * TILE : (t + 1) * TILE, b * TILE : (b + 1) * TILE]
            out[t, b] = front[t, b] - piece

    @pl.when(step == 0)
    def _():
        for t in range(1, LROWS):
            out[t, 0] = own[t]

        @pl.when((at[0] * 4 + at[1]) * 2 + at[2] >= PT)
        def _():
            out[0, 0] = own[0]


def update(at, columns, front, pieces, corner, inverses):
    height = LROWS * TILE
    vmem = pl.BlockSpec(memory_space=pltpu.VMEM)
    block = pl.BlockSpec((LROWS, 2, TILE, TILE), lambda j: (0, j, 0, 0))
    return pl.pallas_call(
        update_kernel,
        grid=(LCOLS // 2,),
        out_shape=jax.ShapeDtypeStruct((LROWS, LCOLS, TILE, TILE), f32),
        in_specs=[
            pl.BlockSpec(memory_space=pltpu.SMEM),
            *(
                pl.BlockSpec((x.shape[0], 1, TILE, TILE), lambda j: (0, j, 0, 0))
                for x in columns
            ),
            *[vmem] * 7,
            block,
            vmem,
        ],
        out_specs=block,
        scratch_shapes=[
            pltpu.VMEM((height, 2 * KP), bf16),
            pltpu.VMEM((2 * TILE, 2 * KP), bf16),
            pltpu.VMEM((2 * TILE, WIDE), f32),
            pltpu.VMEM((LROWS, TILE, TILE), f32),
            pltpu.VMEM((height, PANEL), f32),
            pltpu.VMEM((height, PANEL), f32),
            pltpu.VMEM((PANEL, KP), bf16),
            pltpu.VMEM((KP, PANEL), bf16),
            pltpu.VMEM((PANEL, PANEL), f32),
        ],
        compiler_params=pltpu.CompilerParams(vmem_limit_bytes=26 * MIB),
        cost_estimate=pl.CostEstimate(
            flops=24_000_000_000, bytes_accessed=30 * MIB, transcendentals=0
        ),
        name="update",
    )(at, *columns, *pieces, *corner, front, inverses)


def move(x, axis, size, to):
    return lax.ppermute(x, axis, [(i, to(i)) for i in range(size)])


def both_ways(own, axis):
    up, down = lambda i: (i + 2) % 8, lambda i: (i - 2) % 8
    return [move(own, axis, 8, up), move(own, axis, 8, down)]


def opposite(before, behind, axis):
    half = before.shape[0] // 2
    up, down = lambda i: (i + 2) % 8, lambda i: (i - 2) % 8
    return [move(before[:half], axis, 8, up), move(behind[half:], axis, 8, down)]


def gather_corner(top):
    sib, row = lax.axis_index("sib"), lax.axis_index("row")
    flip = [(4, 2), (5, 3), (6, 0), (7, 1)]
    a = lax.ppermute(top, "sib", [(0, 1)])
    b = lax.ppermute(top, "row", flip)
    c = lax.ppermute(top, ("sib", "row"), [(i, 8 + j) for i, j in flip])
    mine = jnp.where(row >= 4, jnp.where(sib == 0, top, a), jnp.where(sib == 0, b, c))
    return jnp.concatenate([mine, move(mine, "row", 8, lambda i: i ^ 2)], axis=0)


def gather(panel, arrived, landing):
    there = []
    for y in range(4):
        for core in range(2):
            for z in range(4):
                for xh in range(2):
                    to = ((y + z) % 4 * 2 + xh) * 8 + y * 2 + core
                    there.append(((y * 2 + core) * 8 + z * 2 + xh, to))
    across = lax.ppermute(panel, ("row", "col"), there)
    pair = jnp.concatenate([panel, move(panel, "col", 8, lambda i: i ^ 1)], axis=0)
    top = jnp.broadcast_to(panel[:1], (8, TILE, TILE))
    top = lax.all_to_all(top, "col", split_axis=0, concat_axis=0, tiled=True)[:PT]
    pair, top, across = lax.optimization_barrier((pair, top, across))
    pieces = [pair, *both_ways(pair, "col")]
    pieces += opposite(*pieces[1:], "col")
    corner = gather_corner(top)
    pair = jnp.concatenate([across, move(across, "sib", 2, lambda i: 1 - i)], axis=0)
    pair, corner = lax.optimization_barrier((pair, corner))
    columns = [pair, *both_ways(pair, "row")]
    corner = [corner, move(corner, "row", 8, lambda i: i ^ 1)]
    front = add_up(False, arrived, landing)
    *columns, front = lax.optimization_barrier((*columns, front))
    columns += opposite(*columns[1:], "row")
    columns = columns + [move(x, "row", 8, lambda i: i ^ 1) for x in columns]
    columns = [x.reshape(-1, LROWS, TILE, TILE) for x in columns]
    return columns, pieces, corner, front


def local(child_tiles, child_rows, child_slots, tile_count, inverses):
    grid_rows = lax.axis_size("sib") * lax.axis_size("row")
    columns = lax.axis_size("col")
    devices = grid_rows * columns
    slot_ids = child_slots[0, 0]
    live = tile_count[0]
    row_list = child_rows[0]
    child_row, child_col = slot_ids // CHILD_TILES, slot_ids % CHILD_TILES
    positions = jnp.arange(CHILD_TILES, dtype=i32)
    lookup = lambda x: jnp.sum(
        jnp.where(x[:, None] == positions[None, :], row_list[None, :], 0), axis=1
    )
    parent_row, parent_col = lookup(child_row), lookup(child_col)
    owner = parent_row % grid_rows * columns + parent_col % columns
    target = parent_row // grid_rows * LCOLS + parent_col // columns
    order = jnp.arange(slot_ids.shape[0], dtype=i32)
    is_live = order < live
    earlier = (
        (owner[:, None] == owner[None, :])
        & is_live[None, :]
        & (order[None, :] < order[:, None])
    )
    rank = jnp.sum(earlier.astype(i32), axis=1)
    place = jnp.where(is_live, owner * CAP + rank, devices * CAP)
    filled = place[None, :] == jnp.arange(devices * CAP, dtype=i32)[:, None]
    destined = jnp.sum(jnp.where(filled, target[None, :] + 1, 0), axis=1)
    me = lax.axis_index(("sib", "row", "col"))
    mine = jnp.arange(devices, dtype=i32) == me
    meta = jnp.where(mine, destined.reshape(devices, CAP, 1), 0).astype(f32)
    meta = jnp.pad(meta, ((0, 0), (0, META - CAP), (0, 0)))
    outgoing = pack(place, live, child_tiles[0, 0], meta)
    arrived = lax.all_to_all(
        outgoing, ("sib", "row", "col"), split_axis=0, concat_axis=0, tiled=True
    )
    panel, landing = add_up(True, arrived)
    columns, pieces, corner, front = gather(panel, arrived, landing)
    row = lax.axis_index("row")
    col = lax.axis_index("col")
    at = jnp.stack([lax.axis_index("sib"), row // 2, row % 2, col // 2, col % 2])
    at = at.astype(i32)
    out = update(at, columns, front, pieces, corner, inverses)
    return out.reshape(LROWS, 1, LCOLS, 1, TILE, TILE)


def solution(mesh):
    return jax.shard_map(
        local,
        mesh=mesh,
        in_specs=(
            P("sib", ("row", "col"), None, None, None),
            P("sib", None),
            P("sib", ("row", "col"), None),
            P("sib", ("row", "col")),
            P(),
        ),
        out_specs=P(None, ("sib", "row"), None, "col", None, None),
        check_vma=False,
    )
```

```python
import functools

import jax
import jax.numpy as jnp
from jax import lax
from jax.experimental import pallas as pl
from jax.experimental.pallas import tpu as pltpu
from jax.sharding import PartitionSpec as P

NF = 16384
TILE = 128
PANEL = 512
NPANEL = 2
CHILD_TILES = 64
CAP = 2
PT = PANEL // TILE
WIDE = NPANEL * PANEL
META = 8
LROWS, LCOLS = 8, 16
f32, bf16, i32 = jnp.float32, jnp.bfloat16, jnp.int32
MIB = 1 << 20


def split(x):
    hi = x.astype(bf16)
    return hi, (x - hi.astype(f32)).astype(bf16)


def pack_kernel(place, live, tiles, meta, out):
    def put(m, carry):
        d = place[m] // CAP
        k = place[m] % CAP
        out[d, pl.ds(pl.multiple_of(k * TILE, TILE), TILE), :] = tiles[m]
        return carry

    out[:, CAP * TILE :, :] = meta[...]
    lax.fori_loop(0, live[0], put, 0)


def pack(place, live, tiles, meta):
    devices = meta.shape[0]
    vmem = pl.BlockSpec(memory_space=pltpu.VMEM)
    smem = pl.BlockSpec(memory_space=pltpu.SMEM)
    return pl.pallas_call(
        pack_kernel,
        out_shape=jax.ShapeDtypeStruct((devices, CAP * TILE + META, TILE), f32),
        in_specs=[smem, smem, vmem, vmem],
        out_specs=vmem,
        compiler_params=pltpu.CompilerParams(vmem_limit_bytes=16 * MIB),
        name="pack",
    )(place, live, tiles, meta)


def add_kernel(panel, *refs):
    if panel:
        arrived, out, landing, buf, where_to, sem, head, places, head_sem = refs
        slots = arrived.shape[0] * CAP
        copy = pltpu.make_async_copy(arrived.at[:, CAP * TILE :, :], head, head_sem)
        copy.start()
        copy.wait()
        places[...] = jnp.sum(head[...], axis=0).astype(i32) - 1
        copy = pltpu.make_async_copy(places, landing, head_sem)
        copy.start()
        out[...] = jnp.zeros_like(out)
        copy.wait()
    else:
        landing, arrived, out, buf, where_to, sem = refs
        slots = arrived.shape[0] * CAP

    def fetch(k, n):
        pair, turn = k // CAP, k % CAP
        rows = pl.ds(pl.multiple_of(turn * TILE, TILE), TILE)
        return pltpu.make_async_copy(arrived.at[pair, rows, :], buf.at[n], sem)

    def scan(k, n):
        t = landing[k % CAP, k // CAP]
        hit = (t >= 0) & (t % LCOLS == 0) if panel else t >= 0

        @pl.when(hit)
        def _():
            where_to[n] = t
            fetch(k, n).start()

        return n + hit.astype(i32)

    count = lax.fori_loop(0, slots, scan, 0, unroll=8)
    if not panel:
        out[...] = jnp.zeros_like(out)
    lax.fori_loop(0, count, lambda n, c: (fetch(0, n).wait(), c)[1], 0)

    def add(n, c):
        t = where_to[n]
        if panel:
            a = t // LCOLS
            out[a] = out[a] + buf[n]
        else:
            a, b = t // LCOLS, t % LCOLS
            out[a, b] = out[a, b] + buf[n]
        return c

    lax.fori_loop(0, count, add, 0)


def add_up(panel, arrived, landing=None):
    devices = arrived.shape[0]
    vmem = pl.BlockSpec(memory_space=pltpu.VMEM)
    smem = pl.BlockSpec(memory_space=pltpu.SMEM)
    scratch = [
        pltpu.VMEM((devices * CAP, TILE, TILE), f32),
        pltpu.SMEM((devices * CAP,), i32),
        pltpu.SemaphoreType.DMA,
    ]
    any_space = pl.BlockSpec(memory_space=pl.ANY)
    if panel:
        return pl.pallas_call(
            functools.partial(add_kernel, True),
            out_shape=[
                jax.ShapeDtypeStruct((LROWS, TILE, TILE), f32),
                jax.ShapeDtypeStruct((META, devices), i32),
            ],
            in_specs=[any_space],
            out_specs=[vmem, smem],
            scratch_shapes=scratch
            + [
                pltpu.VMEM((devices, META, TILE), f32),
                pltpu.VMEM((META, devices), i32),
                pltpu.SemaphoreType.DMA,
            ],
            compiler_params=pltpu.CompilerParams(vmem_limit_bytes=56 * MIB),
            name="add_panel",
        )(arrived)
    return pl.pallas_call(
        functools.partial(add_kernel, False),
        out_shape=jax.ShapeDtypeStruct((LROWS, LCOLS, TILE, TILE), f32),
        in_specs=[smem, any_space],
        out_specs=vmem,
        scratch_shapes=scratch,
        compiler_params=pltpu.CompilerParams(vmem_limit_bytes=30 * MIB),
        cost_estimate=pl.CostEstimate(
            flops=1000, bytes_accessed=24 * MIB, transcendentals=0
        ),
        name="add_all",
    )(landing, arrived)


BLOCK = 256
KB = 3 * BLOCK
KP = 3 * PANEL


def left_form(ref, lane, x):
    hi, lo = split(x)
    for k in range(x.shape[1] // BLOCK):
        for part, half in enumerate((hi, hi, lo)):
            at = lane + (3 * k + part) * BLOCK
            ref[:, at : at + BLOCK] = half[:, k * BLOCK : (k + 1) * BLOCK]


def right_rows(ref, x):
    hi, lo = split(x)
    for k in range(x.shape[1] // BLOCK):
        for part, half in enumerate((hi, lo, hi)):
            at = (3 * k + part) * BLOCK
            ref[:, at : at + BLOCK] = half[:, k * BLOCK : (k + 1) * BLOCK]


def right_columns(ref, x):
    hi, lo = split(x)
    for k in range(x.shape[0] // BLOCK):
        for part, half in enumerate((hi, lo, hi)):
            at = (3 * k + part) * BLOCK
            ref[at : at + BLOCK, :] = half[k * BLOCK : (k + 1) * BLOCK, :]


def times(a, b):
    return jnp.dot(a, b, preferred_element_type=f32)


def times_transposed(a, b):
    return lax.dot_general(a, b, (((1,), (1,)), ((), ())), preferred_element_type=f32)


def inverse_transposed(x, w):
    return times_transposed(x[:, :KB], w[:BLOCK, :KB]), times_transposed(x[...], w[BLOCK:, :])


def inverse(x, w):
    return times(x[...], w[:, :BLOCK]), times(x[:, KB:], w[KB:, BLOCK:])


def row_factors(at, pieces, corner, inv_hbm, inverses, z, own, f0, f1, left, r_rows, r_cols, low, sems):
    dz, xh = at[3], at[4]
    row = (at[0] * 4 + at[1]) * 2 + at[2]
    col = dz * 2 + xh
    around = lambda d, other: (dz + d + 4) % 4 * 2 + (1 - xh if other else xh)
    here, up, down, far, far2 = pieces
    fetch = pltpu.make_async_copy(inv_hbm, inverses, sems.at[0])
    fetch.start()
    for piece, first, source in (
        (here, 0, around(0, False)),
        (here, 8, around(0, True)),
        (up, 0, around(-1, False)),
        (up, 8, around(-1, True)),
        (down, 0, around(1, False)),
        (down, 8, around(1, True)),
        (far, 0, around(2, False)),
        (far2, 0, around(2, True)),
    ):
        lanes = pl.ds(pl.multiple_of(source % PT * TILE, TILE), TILE)
        rows = pl.ds(first * TILE, LROWS * TILE)
        for panel, ref in enumerate((f0, f1)):

            @pl.when(source // PT == panel)
            def _():
                pltpu.make_async_copy(piece.at[rows, :], ref.at[:, lanes], sems.at[1]).start()

    tile = jnp.where(lax.broadcasted_iota(i32, (LROWS * TILE, 1), 0) < TILE, row, NF)
    my_lanes = pl.ds(pl.multiple_of(col % PT * TILE, TILE), TILE)

    def keep(ref, tiles):
        for a in range(tiles):
            own[a] = ref[a * TILE : (a + 1) * TILE, my_lanes]

    fetch.wait()
    right_rows(r_rows, inverses[0])
    y_bit = jnp.where(at[1] >= 2, at[1], 3 - at[1]) - 2
    for k in range(PT):
        i = (y_bit ^ (k & 1)) * 2 + (at[2] ^ (k >> 1))
        rows = pl.ds(pl.multiple_of(i * TILE, TILE), TILE)
        for j in range(PT):
            low[rows, j * TILE : (j + 1) * TILE] = corner[k >> 1][(k & 1) * PT + j]
    left_form(left.at[:PANEL], 0, low[...])
    one, two = inverse_transposed(left.at[:PANEL], r_rows)
    low[:, :BLOCK] = one
    low[:, BLOCK:] = two
    for _ in range(8):
        lanes = pl.ds(0, TILE)
        rows = pl.ds(0, LROWS * TILE)
        pltpu.make_async_copy(here.at[rows, :], f0.at[:, lanes], sems.at[1]).wait()
    left_form(left, 0, f0[...])
    one, two = inverse_transposed(left, r_rows)
    f0[:, :BLOCK] = jnp.where(tile >= PT, one, 0.0)
    f0[:, BLOCK:] = jnp.where(tile >= PT, two, 0.0)

    @pl.when(col < PT)
    def _():
        keep(f0, LROWS)

    left_form(left, 0, f0[...])
    right_rows(r_rows, low[...])
    f1[...] = f1[...] - times_transposed(left[...], r_rows[...])

    @pl.when(col >= PT)
    def _():
        keep(f1, 1)

    left_form(left, 0, f1[...])
    right_rows(r_rows, inverses[1])
    one, two = inverse_transposed(left, r_rows)
    f1[:, :BLOCK] = jnp.where(tile >= 2 * PT, one, 0.0)
    f1[:, BLOCK:] = jnp.where(tile >= 2 * PT, two, 0.0)

    @pl.when(col >= PT)
    def _():
        for a in range(1, LROWS):
            own[a] = f1[a * TILE : (a + 1) * TILE, my_lanes]

        @pl.when(row >= 2 * PT)
        def _():
            own[0] = f1[:TILE, my_lanes]

    left_form(left, 0, f1[...])
    right_columns(r_cols, inverses[1])
    one, two = inverse(left, r_cols)
    f1[:, :BLOCK] = one
    f1[:, BLOCK:] = two
    left_form(z, KP, f1[...])
    right_columns(r_cols, low[...])
    f0[...] = f0[...] - times(z[:, KP:], r_cols[...])
    left_form(left, 0, f0[...])
    right_columns(r_cols, inverses[0])
    one, two = inverse(left, r_cols)
    f0[:, :BLOCK] = one
    f0[:, BLOCK:] = two
    left_form(z, 0, f0[...])


def update_kernel(
    at, *refs
):
    columns, pieces, corner = refs[:10], refs[10:15], refs[15:17]
    front, inv_hbm, out = refs[17:20]
    z, right, raw, own, f0, f1, r_rows, r_cols, low, inverses, sems = refs[20:]
    left = z.at[:, :KP]
    step = pl.program_id(0)

    @pl.when(step == 0)
    def _():
        row_factors(
            at, pieces, corner, inv_hbm, inverses, z, own, f0, f1, left, r_rows, r_cols, low, sems
        )

    for k in range(2):
        core = at[2] ^ k
        here, up, down, far, far2 = columns[5 * k : 5 * k + 5]
        for ref, n, other, dy in (
            (here, 0, 0, 0),
            (here, 1, 1, 0),
            (up, 0, 0, -1),
            (up, 1, 1, -1),
            (down, 0, 0, 1),
            (down, 1, 1, 1),
            (far, 0, 0, 2),
            (far2, 0, 1, 2),
        ):
            source = (at[1] + dy - at[3] + 8) % 4 * 2 + core
            rows = pl.ds(pl.multiple_of((at[0] ^ other) * TILE, TILE), TILE)
            lanes = pl.ds(pl.multiple_of(source * TILE, TILE), TILE)
            raw[rows, lanes] = ref[n, 0]
    right_rows(right, raw[...])
    change = times_transposed(z[...], right[...])
    for t in range(LROWS):
        for b in range(2):
            piece = change[t * TILE : (t + 1) * TILE, b * TILE : (b + 1) * TILE]
            out[t, b] = front[t, b] - piece

    @pl.when(step == 0)
    def _():
        for t in range(1, LROWS):
            out[t, 0] = own[t]

        @pl.when((at[0] * 4 + at[1]) * 2 + at[2] >= PT)
        def _():
            out[0, 0] = own[0]


def update(at, columns, front, pieces, corner, inverses):
    height = LROWS * TILE
    vmem = pl.BlockSpec(memory_space=pltpu.VMEM)
    block = pl.BlockSpec((LROWS, 2, TILE, TILE), lambda j: (0, j, 0, 0))
    return pl.pallas_call(
        update_kernel,
        grid=(LCOLS // 2,),
        out_shape=jax.ShapeDtypeStruct((LROWS, LCOLS, TILE, TILE), f32),
        in_specs=[
            pl.BlockSpec(memory_space=pltpu.SMEM),
            *(
                pl.BlockSpec((x.shape[0], 1, TILE, TILE), lambda j: (0, j, 0, 0))
                for x in columns
            ),
            *[pl.BlockSpec(memory_space=pl.ANY)] * 5,
            *[vmem] * 2,
            block,
            pl.BlockSpec(memory_space=pl.ANY),
        ],
        out_specs=block,
        scratch_shapes=[
            pltpu.VMEM((height, 2 * KP), bf16),
            pltpu.VMEM((2 * TILE, 2 * KP), bf16),
            pltpu.VMEM((2 * TILE, WIDE), f32),
            pltpu.VMEM((LROWS, TILE, TILE), f32),
            pltpu.VMEM((height, PANEL), f32),
            pltpu.VMEM((height, PANEL), f32),
            pltpu.VMEM((PANEL, KP), bf16),
            pltpu.VMEM((KP, PANEL), bf16),
            pltpu.VMEM((PANEL, PANEL), f32),
            pltpu.VMEM((NPANEL, PANEL, PANEL), f32),
            pltpu.SemaphoreType.DMA((2,)),
        ],
        compiler_params=pltpu.CompilerParams(vmem_limit_bytes=40 * MIB),
        cost_estimate=pl.CostEstimate(
            flops=24_000_000_000, bytes_accessed=30 * MIB, transcendentals=0
        ),
        name="update",
    )(at, *columns, *pieces, *corner, front, inverses)


def move(x, axis, size, to):
    return lax.ppermute(x, axis, [(i, to(i)) for i in range(size)])


def both_ways(own, axis):
    up, down = lambda i: (i + 2) % 8, lambda i: (i - 2) % 8
    return [move(own, axis, 8, up), move(own, axis, 8, down)]


def opposite(before, behind, axis):
    half = before.shape[0] // 2
    up, down = lambda i: (i + 2) % 8, lambda i: (i - 2) % 8
    return [move(before[:half], axis, 8, up), move(behind[half:], axis, 8, down)]


def gather_corner(top):
    sib, row = lax.axis_index("sib"), lax.axis_index("row")
    flip = [(4, 2), (5, 3), (6, 0), (7, 1)]
    a = lax.ppermute(top, "sib", [(0, 1)])
    b = lax.ppermute(top, "row", flip)
    c = lax.ppermute(top, ("sib", "row"), [(i, 8 + j) for i, j in flip])
    mine = jnp.where(row >= 4, jnp.where(sib == 0, top, a), jnp.where(sib == 0, b, c))
    return jnp.concatenate([mine, move(mine, "row", 8, lambda i: i ^ 2)], axis=0)


def gather(panel, arrived, landing):
    there = []
    for y in range(4):
        for core in range(2):
            for z in range(4):
                for xh in range(2):
                    to = ((y + z) % 4 * 2 + xh) * 8 + y * 2 + core
                    there.append(((y * 2 + core) * 8 + z * 2 + xh, to))
    across = lax.ppermute(panel, ("row", "col"), there)
    pair = jnp.concatenate([panel, move(panel, "col", 8, lambda i: i ^ 1)], axis=0)
    top = jnp.broadcast_to(panel[:1], (8, TILE, TILE))
    top = lax.all_to_all(top, "col", split_axis=0, concat_axis=0, tiled=True)[:PT]
    pair, top, across = lax.optimization_barrier((pair, top, across))
    pieces = [pair, *both_ways(pair, "col")]
    pieces += opposite(*pieces[1:], "col")
    corner = gather_corner(top)
    pair = jnp.concatenate([across, move(across, "sib", 2, lambda i: 1 - i)], axis=0)
    pair, corner = lax.optimization_barrier((pair, corner))
    columns = [pair, *both_ways(pair, "row")]
    corner = [corner, move(corner, "row", 8, lambda i: i ^ 1)]
    front = add_up(False, arrived, landing)
    *columns, front = lax.optimization_barrier((*columns, front))
    columns += opposite(*columns[1:], "row")
    columns = columns + [move(x, "row", 8, lambda i: i ^ 1) for x in columns]
    columns = [x.reshape(-1, LROWS, TILE, TILE) for x in columns]
    pieces = [x.reshape(-1, TILE) for x in pieces]
    return columns, pieces, corner, front


def local(child_tiles, child_rows, child_slots, tile_count, inverses):
    grid_rows = lax.axis_size("sib") * lax.axis_size("row")
    columns = lax.axis_size("col")
    devices = grid_rows * columns
    slot_ids = child_slots[0, 0]
    live = tile_count[0]
    row_list = child_rows[0]
    child_row, child_col = slot_ids // CHILD_TILES, slot_ids % CHILD_TILES
    positions = jnp.arange(CHILD_TILES, dtype=i32)
    lookup = lambda x: jnp.sum(
        jnp.where(x[:, None] == positions[None, :], row_list[None, :], 0), axis=1
    )
    parent_row, parent_col = lookup(child_row), lookup(child_col)
    owner = parent_row % grid_rows * columns + parent_col % columns
    target = parent_row // grid_rows * LCOLS + parent_col // columns
    order = jnp.arange(slot_ids.shape[0], dtype=i32)
    is_live = order < live
    earlier = (
        (owner[:, None] == owner[None, :])
        & is_live[None, :]
        & (order[None, :] < order[:, None])
    )
    rank = jnp.sum(earlier.astype(i32), axis=1)
    place = jnp.where(is_live, owner * CAP + rank, devices * CAP)
    filled = place[None, :] == jnp.arange(devices * CAP, dtype=i32)[:, None]
    destined = jnp.sum(jnp.where(filled, target[None, :] + 1, 0), axis=1)
    me = lax.axis_index(("sib", "row", "col"))
    mine = jnp.arange(devices, dtype=i32) == me
    meta = jnp.where(mine, destined.reshape(devices, CAP, 1), 0).astype(f32)
    meta = jnp.pad(meta, ((0, 0), (0, META - CAP), (0, 0)))
    outgoing = pack(place, live, child_tiles[0, 0], meta)
    arrived = lax.all_to_all(
        outgoing, ("sib", "row", "col"), split_axis=0, concat_axis=0, tiled=True
    )
    panel, landing = add_up(True, arrived)
    columns, pieces, corner, front = gather(panel, arrived, landing)
    row = lax.axis_index("row")
    col = lax.axis_index("col")
    at = jnp.stack([lax.axis_index("sib"), row // 2, row % 2, col // 2, col % 2])
    at = at.astype(i32)
    out = update(at, columns, front, pieces, corner, inverses)
    return out.reshape(LROWS, 1, LCOLS, 1, TILE, TILE)


def solution(mesh):
    return jax.shard_map(
        local,
        mesh=mesh,
        in_specs=(
            P("sib", ("row", "col"), None, None, None),
            P("sib", None),
            P("sib", ("row", "col"), None),
            P("sib", ("row", "col")),
            P(),
        ),
        out_specs=P(None, ("sib", "row"), None, "col", None, None),
        check_vma=False,
    )
```
